256 devices in a mesh: node: 16 (over y, x), local: 16 (over z, core).
Axes of the slice: x: 4, y: 4, z: 8, core: 2. Of those that a mesh axis runs over, the one named last changes fastest.
Arguments:
- frames: bfloat16 [262144, 1024], P(('node', 'local')), may hold values from -6 to 6
- lengths: int32 [256, 4], P(('node', 'local')), may hold values from 1 to 256, 768 in all within a row
- routes: int32 [262144, 2], P(('node', 'local')), may hold values from 0 to 63, all different within a row
- owners: int32 [32, 1], replicated, may hold values from 0 to 15; in each aligned block of 32 rows (0 to 31, 32 to 63, ...) at most 6 rows name the same one
- pw_weight: bfloat16 [1024, 2048], replicated, may hold values from -0.1875 to 0.1875
- dw_kernel: bfloat16 [31, 1024], replicated, may hold values from -1 to 1
- conv_grad: bfloat16 [262144, 1024], P(('node', 'local')), may hold values from -6 to 6
- hidden_grad: bfloat16 [256, 24, 4096], P(('node', 'local')), may hold values from -0.1875 to 0.1875
Outputs:
- frame_grad: bfloat16 [262144, 1024], P(('node', 'local'))
- owned_grad: float32 [96, 1024, 128], P('node', 'local')
The draws below stay inside these ranges and needn't reach their ends.
Inputs may be any that keep to these rules, and one draw needn't show every extreme that they name: `routes`: each frame names 2 different experts. The 4 lengths of one device sum to 768, and one of them equals 256. `owners`: no node owns more than 6 blocks and some node owns exactly 6; every node owns one or more.
All inputs are finite; a program needn't handle non-finite values.
Results may differ from the reference program's by a relative error of at most 0.0049.
Values may be sent and summed in bfloat16 or wider, within the bound.
A program may use at most 128 MiB of HBM per device.

```python
import math
import jax
import jax.numpy as jnp
import numpy as np
from jax import lax

D = 1024
FF = 4096
EXPERTS = 64
TOP = 2
KW = 31
UTT = 4
EF = 1
BW = 128
TOK_DEV = 1024
TOKENS = 262144
CAPR = 24
NB = 32
NBLK = 32
CAP = 6
N_NODE = 16
N_LOCAL = 16


def block_scale(key, dims, cuts, least, largest):
    loudness, own = 1.0, jax.random.fold_in(key, 6)
    for dim, blocks in cuts:
        heights = jnp.exp(jax.random.uniform(jax.random.fold_in(own, dim), (blocks,), jnp.float32, least / len(cuts), largest / len(cuts)))
        loudness = loudness * jnp.repeat(heights, dims[dim] // blocks).reshape([-1 if axis == dim else 1 for axis in range(len(dims))])
    return loudness


def picks_of(key, rows, amount, top, lift):
    sequence = jax.random.permutation(jax.random.fold_in(key, 1), amount)
    pull = sequence
    for power in range(3):
        pull = pull * pull // amount
    pull = pull * lift // amount
    tickets = jax.random.randint(jax.random.fold_in(key, 2), (rows, amount), 0, 4096) + pull
    holders = jax.random.permutation(jax.random.fold_in(key, 3), rows)[jnp.arange(amount) % rows]
    tickets = jnp.where(jnp.arange(rows)[:, None] == holders[None, :], 1 << 14, tickets)
    score = tickets * amount + jnp.arange(amount)
    return lax.top_k(score.astype(jnp.int32), top)[1].astype(jnp.int32)


def split_up(count, total, limit, skew):
    portions = [(1 << 20) // math.isqrt(grade ** skew) + 1 for grade in range(2, count + 1)]
    surplus, given = total - limit - (count - 1), [1] * (count - 1)
    while surplus > 0:
        movable = [i for i in range(count - 1) if given[i] < limit]
        mass, budget = sum([portions[i] for i in movable]), surplus
        for i in movable:
            extra = min(limit - given[i], max(1, budget * portions[i] // mass), surplus)
            given[i] = given[i] + extra
            surplus = surplus - extra
    return np.array([limit] + given)


def uneven_parts(key, number_of, total, limit, slope):
    if number_of == 2:
        one = jax.random.randint(key, (), max(1, total - limit), min(limit, total - 1) + 1)
        return jnp.stack([one, total - one])
    sizes = jnp.asarray(split_up(number_of, total, limit, slope), jnp.int32)
    twos = (number_of - 1) // 2
    donor, receiver = sizes[1:1 + 2 * twos:2], sizes[2:2 + 2 * twos:2]
    margin = jnp.minimum(donor - 1, limit - receiver)
    shifted = jax.random.randint(jax.random.fold_in(key, 1), (twos,), 0, 1 << 20) % (margin + 1)
    sizes = sizes.at[1:1 + 2 * twos:2].set(donor - shifted).at[2:2 + 2 * twos:2].set(receiver + shifted)
    return sizes[jax.random.permutation(jax.random.fold_in(key, 2), number_of)]


def assign_block(key, own, number, rows, number_of, top, bound, slope):
    order = jax.random.permutation(key, number_of)
    crowded, ordinary = shares(number_of, rows * top, bound, slope, True), shares(number_of, rows * top, bound, slope, False)
    places = jnp.arange(number_of)

    def named(sizes, turn):
        used = int((sizes > 0).sum())
        fixed = max(1, used // 4)
        shifted = fixed + (places - fixed + turn * (used - fixed)) % max(1, number_of - fixed)
        return jnp.zeros((number_of,), jnp.int32).at[order[jnp.where(places < fixed, places, shifted)]].set(jnp.asarray(sizes, jnp.int32))

    sizes = jnp.where(number % 4 == 0, named(crowded, number // 4), named(ordinary, number - number // 4 - 1))
    mixed = jax.random.permutation(jax.random.fold_in(own, 3), number_of)
    donor, taker = mixed[0:number_of // 2 * 2:2], mixed[1:number_of // 2 * 2:2]
    margin = jnp.minimum(sizes[donor] - 1, bound - sizes[taker]) // 2
    margin = jnp.where((donor == order[0]) | (taker == order[0]) | (sizes[taker] == 0), 0, jnp.maximum(margin, 0))
    shifted = jax.random.randint(jax.random.fold_in(own, 4), (number_of // 2,), 0, 1 << 20) % (margin + 1)
    sizes = sizes.at[donor].add(-shifted).at[taker].add(shifted)
    labels = jnp.searchsorted(jnp.cumsum(sizes), jnp.arange(rows * top), side="right").astype(jnp.int32)
    listing = labels.reshape(top, rows).T
    listing = listing[jax.random.permutation(jax.random.fold_in(own, 1), rows)]
    turn = jax.random.randint(jax.random.fold_in(own, 2), (rows, 1), 0, top)
    return jnp.take_along_axis(listing, (jnp.arange(top)[None, :] + turn) % top, axis=1)


def shares(amount, total, bound, lean, full):
    loads = [(1 << 20) // math.isqrt(grade ** lean) + 1 for grade in range(1, amount + 1)]
    largest = bound if full else min(bound, max(-(-total // amount), total * loads[0] // sum(loads)))
    least = 1 if total - largest >= amount - 1 else 0
    holding, surplus = [largest] + [least] * (amount - 1), total - largest - least * (amount - 1)
    while surplus > 0:
        candidates = [i for i in range(1, amount) if holding[i] < largest] or [i for i in range(1, amount) if holding[i] < bound]
        pool, budget = sum([loads[i] for i in candidates]), surplus
        for i in candidates:
            addition = min(bound - holding[i], max(1, budget * loads[i] // pool), surplus)
            holding[i] = holding[i] + addition
            surplus = surplus - addition
    return np.array(holding)


def scatter_about(rng, extent, spread, reach, cuts=(), kind=jnp.bfloat16):
    values = jax.random.normal(rng, extent, jnp.float32) * spread
    if len(cuts) > 0:
        values = block_scale(rng, extent, cuts, -0.22, 0.18) * values
    return jnp.clip(values, min=-reach, max=reach).astype(kind)


def setup_inputs(seed: int = 0) -> dict:
    keys = jax.random.split(jax.random.key(seed), 9)
    frames = scatter_about(keys[0], (TOKENS, D), 1.0, 6.0, ((0, 256),))
    lengths = jax.vmap(lambda own: uneven_parts(own, UTT, 3 * TOK_DEV // 4, TOK_DEV // UTT, 2))(jax.random.split(keys[1], (N_NODE * N_LOCAL))).reshape((N_NODE * N_LOCAL, UTT)).astype(jnp.int32)
    routes = picks_of(keys[2], TOKENS, EXPERTS, TOP, 0)
    owners_keys = jax.random.split(jax.random.fold_in(keys[3], 1), NBLK // NBLK)
    owners_turns = jax.random.permutation(jax.random.fold_in(keys[3], 3), NBLK // NBLK)
    owners = jax.vmap(lambda own, number: assign_block(jax.random.fold_in(keys[3], 2), own, number, NBLK, N_NODE, 1, CAP, 2))(owners_keys, owners_turns).reshape((NBLK, 1))
    pw_weight = scatter_about(keys[4], (D, 2 * D), D ** -0.5, 0.1875)
    dw_kernel = scatter_about(keys[5], (KW, D), KW ** -0.5, 1.0)
    conv_grad = scatter_about(keys[6], (TOKENS, D), 1.0, 6.0, ((0, 256),))
    hidden_grad = scatter_about(keys[7], (N_NODE * N_LOCAL * EF, CAPR, FF), ((CAPR * N_NODE * N_LOCAL) ** -0.5), 0.1875, ((0, 256),))
    return {"frames": frames, "lengths": lengths, "routes": routes, "owners": owners, "pw_weight": pw_weight, "dw_kernel": dw_kernel, "conv_grad": conv_grad, "hidden_grad": hidden_grad}


def frame_valid(length_row, frame_count):
    utt_len = frame_count // UTT
    position = jnp.arange(frame_count, dtype=jnp.int32)
    utterance_of = position // utt_len
    utt_limit = jnp.sum(jnp.where(utterance_of[:, None] == jnp.arange(UTT, dtype=jnp.int32)[None, :], length_row[None, :], 0), axis=1)
    return (position % utt_len) < utt_limit


def depthwise_back(upstream, kernel, valid_mask):
    frame_count, model_width = upstream.shape
    half_width = (KW - 1) // 2
    utt_len = frame_count // UTT
    masked = jnp.where(valid_mask[:, None], upstream.astype(jnp.float32), 0.0)
    utterances = masked.reshape(UTT, utt_len, model_width)
    padded = jnp.pad(utterances, ((0, 0), (half_width, half_width), (0, 0)))
    kernel_f = kernel.astype(jnp.float32)
    running = jnp.zeros((UTT, utt_len, model_width), jnp.float32)
    for offset in range(KW):
        begin = 2 * half_width - offset
        running = running + kernel_f[offset] * padded[:, begin:begin + utt_len]
    return jnp.where(valid_mask[:, None], running.reshape(frame_count, model_width), 0.0)


def conv_branch(frames, pw_weight, conv_grad, dw_kernel, valid_mask):
    model_width = frames.shape[1]
    projected = jnp.dot(frames, pw_weight, preferred_element_type=jnp.float32)
    glu_value = projected[:, :model_width]
    glu_gate = projected[:, model_width:]
    conv_back = depthwise_back(conv_grad, dw_kernel, valid_mask)
    gate_sig = jax.nn.sigmoid(glu_gate)
    d_proj = jnp.concatenate([conv_back * gate_sig, conv_back * glu_value * gate_sig * (1.0 - gate_sig)], axis=1).astype(jnp.bfloat16)
    out = lax.dot_general(d_proj, pw_weight, (((1,), (1,)), ((), ())), preferred_element_type=jnp.float32)
    return out.astype(jnp.bfloat16)


def slot_selector(routes, valid_mask, capacity):
    expert_ids = jnp.arange(EF, dtype=jnp.int32)
    routed_here = jnp.any(routes[:, :, None] == expert_ids[None, None, :], axis=1) & valid_mask[:, None]
    slot_order = jnp.cumsum(routed_here.astype(jnp.int32), axis=0) - 1
    slot_index = jnp.arange(capacity, dtype=jnp.int32)
    chosen = routed_here.T[:, None, :] & (slot_order.T[:, None, :] == slot_index[None, :, None])
    return chosen


def reference(frames, lengths, routes, owners, pw_weight, dw_kernel, conv_grad, hidden_grad):
    frames_b = frames.reshape(N_NODE, N_LOCAL, TOK_DEV, D)
    lengths_b = lengths.reshape(N_NODE, N_LOCAL, UTT)
    routes_b = routes.reshape(N_NODE, N_LOCAL, TOK_DEV, TOP)
    conv_b = conv_grad.reshape(N_NODE, N_LOCAL, TOK_DEV, D)
    hidden_b = hidden_grad.reshape(N_NODE, N_LOCAL, EF, CAPR, FF)

    def device_step(node_total, pieces):
        frame_part, length_part, route_part, conv_part, hidden_part = pieces
        valid_mask = frame_valid(length_part, TOK_DEV)
        out_part = conv_branch(frame_part, pw_weight, conv_part, dw_kernel, valid_mask)
        chosen = slot_selector(route_part, valid_mask, CAPR).astype(jnp.float32)
        slot_frames = jnp.einsum('est,td->esd', chosen, frame_part.astype(jnp.float32)).astype(jnp.bfloat16)
        partial_value = jnp.einsum('esd,esf->edf', slot_frames.astype(jnp.float32), hidden_part.astype(jnp.float32))
        return node_total + partial_value, out_part

    def node_step(running, pieces):
        node_total, outs = lax.scan(device_step, jnp.zeros((EF, D, FF), jnp.float32), pieces)
        return running + node_total, outs

    total, outs = lax.scan(node_step, jnp.zeros((EF, D, FF), jnp.float32), (frames_b, lengths_b, routes_b, conv_b, hidden_b))
    frame_grad = outs.reshape(TOKENS, D)
    block_data = total.reshape(EF, D, NB, BW).transpose(0, 2, 1, 3).reshape(NBLK, D, BW)
    block_owner = owners[:, 0]
    block_ids = jnp.arange(NBLK, dtype=jnp.int32)
    earlier = (block_owner[:, None] == block_owner[None, :]) & (block_ids[:, None] > block_ids[None, :])
    owner_rank = jnp.sum(earlier.astype(jnp.int32), axis=1)
    target_row = block_owner * CAP + owner_rank
    placement = (jnp.arange(N_NODE * CAP, dtype=jnp.int32)[:, None] == target_row[None, :]).astype(jnp.float32)
    owned_grad = jnp.einsum('ri,idb->rdb', placement, block_data, precision=lax.Precision.HIGHEST)
    return frame_grad, owned_grad
```

```python
import functools

import jax
import jax.numpy as jnp
from jax import lax
from jax.experimental import pallas as pl
from jax.experimental.pallas import tpu as pltpu
from jax.sharding import PartitionSpec as P

MESH = pl.DeviceIdType.MESH
F32, BF16, I32 = jnp.float32, jnp.bfloat16, jnp.int32

TILE = 128
UTT_LEN = 256
KW = 31
CAPR = 24
CHUNKS = 2
CAP = 6


def kernel(
    slots,
    lengths, owners, routes, frames, hidden, weight, taps_hbm, conv_grad,
    out, owned,
    frames_v, hidden_v, weight_v, taps_v, conv_v, out_v, owned_v,
    flags, glu, padded, dproj,
    send1, recv1, piece, piece_b, recv2, half_b, recv3, total_b, gathered,
    load_sem, store_sem,
    send1_sem, recv1_sem, send2_sem, recv2_sem, send3_sem, recv3_sem, send4_sem, recv4_sem,
):
    node, local = lax.axis_index("node"), lax.axis_index("local")
    z, core = local // 2, local % 2
    partner = local + 1 - 2 * core

    def loads():
        yield frames, frames_v, 0
        yield hidden.at[0], hidden_v, 1
        yield taps_hbm, taps_v, 2
        yield conv_grad, conv_v, 3
        for cb in range(8):
            for part in range(2):
                yield (
                    weight.at[:, pl.ds(part * 1024 + cb * TILE, TILE)],
                    weight_v.at[:, pl.ds(cb * 256 + part * TILE, TILE)],
                    4 + cb * 2 + part,
                )

    copies = [pltpu.make_async_copy(s, d, load_sem.at[i]) for s, d, i in loads()]
    for copy in copies:
        copy.start()

    barrier = pltpu.get_barrier_semaphore()

    def greet(o, c):
        pl.semaphore_signal(barrier, inc=1, device_id=((node + o) % 16, local), device_id_type=MESH)
        return c

    def greet_z(o, c):
        pl.semaphore_signal(
            barrier, inc=1, device_id=(node, (z + o) % 8 * 2 + core), device_id_type=MESH
        )
        return c

    lax.fori_loop(1, 16, greet, 0)
    lax.fori_loop(1, 8, greet_z, 0)
    pl.semaphore_signal(barrier, inc=1, device_id=(node, partner), device_id_type=MESH)

    lane = lax.broadcasted_iota(I32, (1, TILE), 1)
    for r in range(8):
        named = routes[:, r * TILE:(r + 1) * TILE] == 0
        named = jnp.max(named.astype(I32), axis=0, keepdims=True)
        valid = lane + (r % 2) * TILE < lengths[0, r // 2]
        flags[r:r + 1, :] = jnp.where(valid, named, 0).astype(F32)
    routed = flags[...]
    upto = (
        lax.broadcasted_iota(I32, (TILE, TILE), 0) <= lax.broadcasted_iota(I32, (TILE, TILE), 1)
    ).astype(F32)
    before = (
        lax.broadcasted_iota(I32, (8, 8), 1) < lax.broadcasted_iota(I32, (8, 8), 0)
    ).astype(F32)
    in_row = jnp.dot(routed, upto, preferred_element_type=F32)
    row_sum = jnp.broadcast_to(jnp.sum(routed, axis=1, keepdims=True), (8, TILE))
    order = in_row + jnp.dot(before, row_sum, preferred_element_type=F32)
    flags[...] = jnp.where(routed > 0, order - 1.0, -1.0)
    want = lax.broadcasted_iota(I32, (32, TILE), 0).astype(F32)
    chosen = jnp.concatenate(
        [(jnp.broadcast_to(flags[r:r + 1, :], (32, TILE)) == want).astype(F32) for r in range(8)], axis=1
    ).astype(BF16)
    copies[0].wait()
    slot = jnp.dot(chosen, frames_v[...], preferred_element_type=F32)[0:CAPR]

    group = lax.broadcasted_iota(I32, (CAPR, TILE), 1) // 32
    sets = []
    for g in range(2):
        tiles = []
        for c in range(2):
            for half in range(2):
                tile = None
                for i in range(4):
                    zz = half * 4 + i
                    part = pltpu.roll(slot[:, zz * TILE:(zz + 1) * TILE], ((i - (2 * c + g)) * 32) % TILE, 1)
                    tile = part if tile is None else jnp.where(group == i, part, tile)
                tiles.append(tile)
        sets.append(jnp.concatenate(tiles, axis=0).astype(BF16))
    copies[1].wait()
    for m in range(8):
        columns = [
            hidden_v[:, (m * 4 + t) * TILE:(m * 4 + t + 1) * TILE].astype(F32) for t in range(4)
        ]
        columns = jnp.concatenate(columns, axis=0).astype(BF16)
        for g in range(2):
            send1[g * 8 + m, 0:96, :] = sets[g]
            send1[g * 8 + m, 96:192, :] = columns
    recv1[node] = send1[node]

    pl.semaphore_wait(barrier, 23)

    rows1 = ((0, 144), (144, 48))

    def copy1(chunk, o):
        to = (node + o) % 16
        rows = pl.ds(*rows1[chunk])
        return pltpu.make_async_remote_copy(
            src_ref=send1.at[to, rows], dst_ref=recv1.at[node, rows],
            send_sem=send1_sem.at[chunk, o], recv_sem=recv1_sem.at[chunk, o],
            device_id=(to, local), device_id_type=MESH,
        )

    def copy2(chunk):
        return pltpu.make_async_remote_copy(
            src_ref=piece_b.at[chunk, 1 - core], dst_ref=recv2.at[chunk],
            send_sem=send2_sem.at[chunk], recv_sem=recv2_sem.at[chunk],
            device_id=(node, partner), device_id_type=MESH,
        )

    def copy3(chunk, o):
        to = (z + o) % 8
        return pltpu.make_async_remote_copy(
            src_ref=half_b.at[chunk, to], dst_ref=recv3.at[chunk, z],
            send_sem=send3_sem.at[chunk, o], recv_sem=recv3_sem.at[chunk, o],
            device_id=(node, to * 2 + core), device_id_type=MESH,
        )

    def copy4(chunk, o):
        to = (node + o) % 16
        return pltpu.make_async_remote_copy(
            src_ref=total_b.at[chunk], dst_ref=gathered.at[node, pl.ds(2 * chunk, 2)],
            send_sem=send4_sem.at[chunk, o], recv_sem=recv4_sem.at[chunk, o],
            device_id=(to, local), device_id_type=MESH,
        )

    def each(count, do):
        def step(o, c):
            do(o)
            return c

        lax.fori_loop(1, count, step, 0)

    for chunk in range(CHUNKS):
        each(16, lambda o: copy1(chunk, o).start())

    def multiply(chunk):
        each(16, lambda o: copy1(chunk, o).wait_recv())

        def tiles(first, count):
            rows = recv1[:, first * CAPR:(first + count) * CAPR, :].astype(F32)
            rows = rows.reshape(16, count, CAPR, TILE)
            parts = [rows[:, t].reshape(16 * CAPR, TILE) for t in range(count)]
            return jnp.concatenate(parts, axis=1).astype(BF16)

        left, right = tiles(0, 4), tiles(4 + 2 * chunk, 2)
        both = lax.dot_general(left, right, (((0,), (0,)), ((), ())), preferred_element_type=F32)
        both = both.reshape(2, 256, 256)
        piece[chunk] = both
        piece_b[chunk] = both.astype(BF16)
        copy2(chunk).start()

    def add_cores(chunk):
        copy2(chunk).wait_recv()
        half = piece[chunk, core] + recv2[chunk].astype(F32)
        half_b[chunk] = half.astype(BF16).reshape(8, 32, 256)
        recv3[chunk, z] = half_b[chunk, z]
        each(8, lambda o: copy3(chunk, o).start())

    def add_chips(chunk):
        each(8, lambda o: copy3(chunk, o).wait_recv())
        total = recv3[chunk, 0].astype(F32)
        for other in range(1, 8):
            total = total + recv3[chunk, other].astype(F32)
        total = total.astype(BF16)
        for t in range(2):
            total_b[chunk, t] = total[:, t * TILE:(t + 1) * TILE]
        for t in range(2):
            gathered[node, 2 * chunk + t] = total_b[chunk, t]
        each(16, lambda o: copy4(chunk, o).start())

    steps = {
        slots[0]: lambda: multiply(0),
        slots[1]: lambda: multiply(1),
        slots[2]: lambda: add_cores(0),
        slots[3]: lambda: add_cores(1),
        slots[4]: lambda: add_chips(0),
        slots[5]: lambda: add_chips(1),
    }

    def hook(now):
        for at, step in steps.items():
            pl.when(now == at)(step)

    padded[0:16, :] = jnp.zeros((16, TILE), F32)
    padded[272:288, :] = jnp.zeros((16, TILE), F32)
    for copy in copies[2:]:
        copy.wait()
    R = 64

    def conv_tile(u, cb):
        rows_u = pl.multiple_of(u * UTT_LEN, UTT_LEN)
        lanes = pl.ds(pl.multiple_of(cb * TILE, TILE), TILE)
        valid = lax.broadcasted_iota(I32, (UTT_LEN, TILE), 0) < lengths[0, u]
        padded[16:272, :] = jnp.where(valid, conv_v[pl.ds(rows_u, UTT_LEN), lanes].astype(F32), 0.0)
        taps = taps_v[:, lanes].astype(F32)
        for r in range(UTT_LEN // R):
            rows = pl.ds(pl.multiple_of(rows_u + r * R, R), R)
            acc = jnp.zeros((R, TILE), F32)
            for k in range(KW):
                first = r * R + KW - k
                acc = acc + taps[k:k + 1, :] * padded[first:first + R, :]
            acc = jnp.where(valid[r * R:(r + 1) * R], acc, 0.0)
            value, gate = glu[rows, 0:TILE], glu[rows, TILE:2 * TILE]
            sig = jax.nn.sigmoid(gate)
            d_value = acc * sig
            d_gate = d_value * value * (1.0 - sig)
            at = pl.multiple_of(cb * 256, 256)
            dproj[rows, pl.ds(at, TILE)] = d_value.astype(BF16)
            dproj[rows, pl.ds(at + TILE, TILE)] = d_gate.astype(BF16)

    def channels(cb, c):
        columns = pl.ds(pl.multiple_of(cb * 256, 256), 256)
        glu[...] = jnp.dot(frames_v[...], weight_v[:, columns], preferred_element_type=F32)

        def utterance(u, c):
            conv_tile(u, cb)
            hook(cb * 4 + u)
            return c

        return lax.fori_loop(0, 4, utterance, c)

    lax.fori_loop(0, 8, channels, 0)

    def store(i):
        columns = pl.ds(pl.multiple_of(i * 256, 256), 256)
        return pltpu.make_async_copy(out_v.at[:, columns], out.at[:, columns], store_sem.at[i])

    def back(i, c):
        columns = pl.ds(pl.multiple_of(i * 256, 256), 256)
        out_v[:, columns] = lax.dot_general(
            dproj[...], weight_v[columns, :], (((1,), (1,)), ((), ())), preferred_element_type=F32
        ).astype(BF16)
        store(i).start()
        hook(32 + i)
        return c

    lax.fori_loop(0, 4, back, 0)

    picks = [jnp.int32(-1)] * CAP
    held = jnp.int32(0)
    for i in range(32):
        mine = owners[i] == node
        picks = [jnp.where(mine & (held == k), i, picks[k]) for k in range(CAP)]
        held = held + mine.astype(I32)
    for chunk in range(CHUNKS):
        each(16, lambda o: copy4(chunk, o).wait_recv())
    for k in range(CAP):
        block = jnp.maximum(picks[k], 0)
        keep = jnp.broadcast_to(picks[k] >= 0, (32, TILE))
        for g in range(2):
            rows = gathered[g * 8 + block // 4, block % 4].astype(F32)
            owned_v[k, g * 32:(g + 1) * 32, :] = jnp.where(keep, rows, 0.0)
    last = pltpu.make_async_copy(owned_v, owned, load_sem.at[0])
    last.start()

    for chunk in range(CHUNKS):
        each(16, lambda o: copy1(chunk, o).wait_send())
        copy2(chunk).wait_send()
        each(8, lambda o: copy3(chunk, o).wait_send())
        each(16, lambda o: copy4(chunk, o).wait_send())
    for i in range(4):
        store(i).wait()
    last.wait()


SLOTS = (13, 17, 16, 20, 23, 28)


def shards(frames, lengths, routes, owners, pw_weight, dw_kernel, conv_grad, hidden_grad):
    smem = pl.BlockSpec(memory_space=pltpu.SMEM)
    vmem = pl.BlockSpec(memory_space=pltpu.VMEM)
    hbm = pl.BlockSpec(memory_space=pl.ANY)
    dma = pltpu.SemaphoreType.DMA
    return pl.pallas_call(
        functools.partial(kernel, SLOTS),
        out_shape=(
            jax.ShapeDtypeStruct((1024, 1024), BF16),
            jax.ShapeDtypeStruct((CAP, 64, TILE), F32),
        ),
        in_specs=[smem, smem, vmem, hbm, hbm, hbm, hbm, hbm],
        out_specs=(hbm, hbm),
        scratch_shapes=[
            pltpu.VMEM((1024, 1024), BF16),
            pltpu.VMEM((CAPR, 4096), BF16),
            pltpu.VMEM((1024, 2048), BF16),
            pltpu.VMEM((KW, 1024), BF16),
            pltpu.VMEM((1024, 1024), BF16),
            pltpu.VMEM((1024, 1024), BF16),
            pltpu.VMEM((CAP, 64, TILE), F32),
            pltpu.VMEM((8, TILE), F32),
            pltpu.VMEM((1024, 256), F32),
            pltpu.VMEM((288, TILE), F32),
            pltpu.VMEM((1024, 2048), BF16),
            pltpu.VMEM((16, 192, TILE), BF16),
            pltpu.VMEM((16, 192, TILE), BF16),
            pltpu.VMEM((CHUNKS, 2, 256, 256), F32),
            pltpu.VMEM((CHUNKS, 2, 256, 256), BF16),
            pltpu.VMEM((CHUNKS, 256, 256), BF16),
            pltpu.VMEM((CHUNKS, 8, 32, 256), BF16),
            pltpu.VMEM((CHUNKS, 8, 32, 256), BF16),
            pltpu.VMEM((CHUNKS, 2, 32, TILE), BF16),
            pltpu.VMEM((16, 4, 32, TILE), BF16),
            dma((20,)), dma((4,)),
            dma((CHUNKS, 16)), dma((CHUNKS, 16)),
            dma((CHUNKS,)), dma((CHUNKS,)),
            dma((CHUNKS, 8)), dma((CHUNKS, 8)),
            dma((CHUNKS, 16)), dma((CHUNKS, 16)),
        ],
        compiler_params=pltpu.CompilerParams(
            collective_id=0, has_side_effects=True, vmem_limit_bytes=56 * 2**20
        ),
    )(
        lengths, owners.reshape(32), routes.T, frames, hidden_grad, pw_weight, dw_kernel, conv_grad
    )


def solution(mesh):
    in_specs = (
        P(("node", "local"), None),
        P(("node", "local"), None),
        P(("node", "local"), None),
        P(),
        P(),
        P(),
        P(("node", "local"), None),
        P(("node", "local"), None, None),
    )
    out_specs = (P(("node", "local"), None), P("node", "local", None))
    return jax.shard_map(shards, mesh=mesh, in_specs=in_specs, out_specs=out_specs, check_vma=False)
```

```python
import functools

import jax
import jax.numpy as jnp
from jax import lax
from jax.experimental import pallas as pl
from jax.experimental.pallas import tpu as pltpu
from jax.sharding import PartitionSpec as P

MESH = pl.DeviceIdType.MESH
F32, BF16, I32 = jnp.float32, jnp.bfloat16, jnp.int32

TILE = 128
UTT_LEN = 256
KW = 31
FAR_FIRST = sorted(range(1, 16), key=lambda o: -min(o // 4, 4 - o // 4) - min(o % 4, 4 - o % 4))
CAPR = 24
CHUNKS = 2
CAP = 6


def kernel(
    slots,
    lengths_hbm, routes_hbm, frames, hidden, weight, taps_hbm, conv_grad,
    out, gathered,
    lengths, routes, frames_v, hidden_v, weight_v, taps_v, conv_v, out_v,
    flags, glu, padded, taps_f, coef, phase, conv_back, dproj,
    send1, recv1, piece, piece_b, recv2, half_b, recv3, total_b,
    load_sem, store_sem,
    send1_sem, recv1_sem, send2_sem, recv2_sem, send3_sem, recv3_sem, send4_sem, recv4_sem,
):
    node, local = lax.axis_index("node"), lax.axis_index("local")
    z, core = local // 2, local % 2
    partner = local + 1 - 2 * core
    y, x = node // 4, node % 4

    def load(source, target, i):
        return pltpu.make_async_copy(source, target, load_sem.at[i])

    def load_weight(cb, part):
        start = pl.multiple_of(cb * TILE, TILE)
        return load(
            weight.at[:, pl.ds(part * 1024 + start, TILE)],
            weight_v.at[:, pl.ds(pl.multiple_of(cb * 256, 256) + part * TILE, TILE)],
            4 + cb * 2 + part,
        )

    load_frames = load(frames, frames_v, 0)
    load_hidden = load(hidden.at[0], hidden_v, 1)
    load_taps = load(taps_hbm, taps_v, 2)
    load_conv = load(conv_grad, conv_v, 3)
    load_lengths = load(lengths_hbm, lengths, 20)
    load_routes = load(routes_hbm, routes, 21)
    load_routes.start()
    load_lengths.start()
    load_frames.start()
    load_hidden.start()

    barrier = pltpu.get_barrier_semaphore()

    def greet(o, c):
        pl.semaphore_signal(barrier, inc=1, device_id=((node + o) % 16, local), device_id_type=MESH)
        return c

    def greet_z(o, c):
        pl.semaphore_signal(
            barrier, inc=1, device_id=(node, (z + o) % 8 * 2 + core), device_id_type=MESH
        )
        return c

    lax.fori_loop(1, 16, greet, 0)
    lax.fori_loop(1, 8, greet_z, 0)
    pl.semaphore_signal(barrier, inc=1, device_id=(node, partner), device_id_type=MESH)

    load_routes.wait()
    load_lengths.wait()
    lane = lax.broadcasted_iota(I32, (1, TILE), 1)
    for r in range(8):
        named = routes[:, r * TILE:(r + 1) * TILE] == 0
        named = jnp.max(named.astype(I32), axis=0, keepdims=True)
        valid = lane + (r % 2) * TILE < lengths[0, r // 2]
        flags[r:r + 1, :] = jnp.where(valid, named, 0).astype(F32)
    routed = flags[...]
    upto = (
        lax.broadcasted_iota(I32, (TILE, TILE), 0) <= lax.broadcasted_iota(I32, (TILE, TILE), 1)
    ).astype(F32)
    before = (
        lax.broadcasted_iota(I32, (8, 8), 1) < lax.broadcasted_iota(I32, (8, 8), 0)
    ).astype(F32)
    in_row = jnp.dot(routed, upto, preferred_element_type=F32)
    row_sum = jnp.broadcast_to(jnp.sum(routed, axis=1, keepdims=True), (8, TILE))
    order = in_row + jnp.dot(before, row_sum, preferred_element_type=F32)
    flags[...] = jnp.where(routed > 0, order - 1.0, -1.0)
    want = lax.broadcasted_iota(I32, (32, TILE), 0).astype(F32)
    chosen = jnp.concatenate(
        [(jnp.broadcast_to(flags[r:r + 1, :], (32, TILE)) == want).astype(F32) for r in range(8)], axis=1
    ).astype(BF16)
    load_frames.wait()
    slot = jnp.dot(chosen, frames_v[...], preferred_element_type=F32)[0:CAPR]

    group = lax.broadcasted_iota(I32, (CAPR, TILE), 1) // 32
    sets = []
    for g in range(2):
        tiles = []
        for c in range(2):
            for half in range(2):
                tile = None
                for i in range(4):
                    zz = half * 4 + i
                    part = pltpu.roll(slot[:, zz * TILE:(zz + 1) * TILE], ((i - (2 * c + g)) * 32) % TILE, 1)
                    tile = part if tile is None else jnp.where(group == i, part, tile)
                tiles.append(tile)
        sets.append(jnp.concatenate(tiles, axis=0).astype(BF16))
    load_hidden.wait()
    for m in range(8):
        columns = [
            hidden_v[:, (m * 4 + t) * TILE:(m * 4 + t + 1) * TILE].astype(F32) for t in range(4)
        ]
        columns = jnp.concatenate(columns, axis=0).astype(BF16)
        for g in range(2):
            send1[g * 8 + m, 0:96, :] = sets[g]
            send1[g * 8 + m, 96:192, :] = columns
    recv1[node] = send1[node]

    pl.semaphore_wait(barrier, 23)

    rows1 = ((0, 144), (144, 48))

    def copy1(chunk, o):
        to = (y + o // 4) % 4 * 4 + (x + o % 4) % 4
        rows = pl.ds(*rows1[chunk])
        return pltpu.make_async_remote_copy(
            src_ref=send1.at[to, rows], dst_ref=recv1.at[node, rows],
            send_sem=send1_sem.at[chunk, o], recv_sem=recv1_sem.at[chunk, o],
            device_id=(to, local), device_id_type=MESH,
        )

    def copy2(chunk):
        return pltpu.make_async_remote_copy(
            src_ref=piece_b.at[chunk, 1 - core], dst_ref=recv2.at[chunk],
            send_sem=send2_sem.at[chunk], recv_sem=recv2_sem.at[chunk],
            device_id=(node, partner), device_id_type=MESH,
        )

    def copy3(chunk, o):
        to = (z + o) % 8
        return pltpu.make_async_remote_copy(
            src_ref=half_b.at[chunk, to], dst_ref=recv3.at[chunk, z],
            send_sem=send3_sem.at[chunk, o], recv_sem=recv3_sem.at[chunk, o],
            device_id=(node, to * 2 + core), device_id_type=MESH,
        )

    def copy4(chunk, o):
        to = (y + o // 4) % 4 * 4 + (x + o % 4) % 4
        return pltpu.make_async_remote_copy(
            src_ref=total_b.at[chunk], dst_ref=gathered.at[node, pl.ds(2 * chunk, 2)],
            send_sem=send4_sem.at[chunk, o], recv_sem=recv4_sem.at[chunk, o],
            device_id=(to, local), device_id_type=MESH,
        )

    def keep_own(chunk):
        return pltpu.make_async_copy(
            total_b.at[chunk], gathered.at[node, pl.ds(2 * chunk, 2)], load_sem.at[chunk]
        )

    def each(count, do):
        def step(o, c):
            do(o)
            return c

        lax.fori_loop(1, count, step, 0)

    for o in FAR_FIRST:
        copy1(0, o).start()
    load_weight(0, 0).start()
    load_weight(0, 1).start()
    load_weight(1, 0).start()
    load_weight(1, 1).start()
    load_taps.start()
    load_conv.start()
    for cb in range(2, 8):
        load_weight(cb, 0).start()
        load_weight(cb, 1).start()


    def send_rest():
        each(16, lambda o: copy1(0, o).wait_send())
        for o in FAR_FIRST:
            copy1(1, o).start()

    def multiply(chunk):
        each(16, lambda o: copy1(chunk, o).wait_recv())

        def tiles(first, count):
            rows = recv1[:, first * CAPR:(first + count) * CAPR, :].astype(F32)
            rows = rows.reshape(16, count, CAPR, TILE)
            parts = [rows[:, t].reshape(16 * CAPR, TILE) for t in range(count)]
            return jnp.concatenate(parts, axis=1).astype(BF16)

        left, right = tiles(0, 4), tiles(4 + 2 * chunk, 2)
        both = lax.dot_general(left, right, (((0,), (0,)), ((), ())), preferred_element_type=F32)
        both = both.reshape(2, 256, 256)
        piece[chunk] = both
        piece_b[chunk] = both.astype(BF16)
        copy2(chunk).start()

    def add_cores(chunk):
        copy2(chunk).wait_recv()
        half = piece[chunk, core] + recv2[chunk].astype(F32)
        half_b[chunk] = half.astype(BF16).reshape(8, 32, 256)
        recv3[chunk, z] = half_b[chunk, z]
        for o in (4, 3, 5, 2, 6, 1, 7):
            copy3(chunk, o).start()

    def add_chips(chunk):
        each(8, lambda o: copy3(chunk, o).wait_recv())
        total = recv3[chunk, 0].astype(F32)
        for other in range(1, 8):
            total = total + recv3[chunk, other].astype(F32)
        total = total.astype(BF16)
        for t in range(2):
            total_b[chunk, t] = total[:, t * TILE:(t + 1) * TILE]
        keep_own(chunk).start()
        for o in FAR_FIRST:
            copy4(chunk, o).start()

    steps = {
        slots[6]: send_rest,
        slots[0]: lambda: multiply(0),
        slots[1]: lambda: multiply(1),
        slots[2]: lambda: add_cores(0),
        slots[3]: lambda: add_cores(1),
        slots[4]: lambda: add_chips(0),
        slots[5]: lambda: add_chips(1),
    }

    def hook(now):
        for at, step in steps.items():
            pl.when(now == at)(step)

    padded[0:16, :] = jnp.zeros((16, TILE), F32)
    padded[272:304, :] = jnp.zeros((32, TILE), F32)
    taps_f[...] = jnp.zeros((40, TILE), F32)
    load_taps.wait()
    load_conv.wait()
    R = 64
    Q = UTT_LEN // 4

    def coefficients(cb):
        taps_f[1:KW + 1, :] = taps_v[:, pl.ds(pl.multiple_of(cb * TILE, TILE), TILE)].astype(F32)
        u0, u1, u2, u3 = (taps_f[pl.ds(3 - m, 8, stride=4), :] for m in range(4))
        filters = (u0 + u1 + u2 + u3, u0 + u1, u2 + u3, u0 + u2, u0, u2, u1 + u3, u1, u3)
        for i, rows in enumerate(filters):
            coef[i * 8:i * 8 + 8, :] = rows

    def conv_tile(u, cb, at):
        rows_u = pl.multiple_of(u * UTT_LEN, UTT_LEN)
        lanes = pl.ds(pl.multiple_of(cb * TILE, TILE), TILE)
        valid = lax.broadcasted_iota(I32, (UTT_LEN, TILE), 0) < lengths[0, u]
        padded[16:272, :] = jnp.where(valid, conv_v[pl.ds(rows_u, UTT_LEN), lanes].astype(F32), 0.0)
        x0, x1, x2, x3, x4, x5, x6 = (padded[pl.ds(1 + m, Q + 8, stride=4), :] for m in range(7))
        d0, d1, d2 = x0 - x1, x2 - x3, x4 - x5
        e0, e1, e2 = x2 - x1, x4 - x3, x6 - x5
        inputs = (x3, x1 - x3, x5 - x3, d1, d0 - d1, d2 - d1, e1, e0 - e1, e2 - e1)
        for i, rows in enumerate(inputs):
            phase[i] = rows

        def correlate(i):
            acc = None
            for j in range(8):
                term = coef[i * 8 + 7 - j:i * 8 + 8 - j, :] * phase[i, j:j + Q, :]
                acc = term if acc is None else acc + term
            return acc

        q0, q1, q2 = correlate(0), correlate(1), correlate(2)
        qa, qb = q0 + q1, q0 + q2
        r0, r1, r2 = correlate(3), correlate(4), correlate(5)
        conv_back[pl.ds(0, Q, stride=4), :] = qa + (r0 + r1)
        conv_back[pl.ds(2, Q, stride=4), :] = qb + (r0 + r2)
        t0, t1, t2 = correlate(6), correlate(7), correlate(8)
        conv_back[pl.ds(1, Q, stride=4), :] = qa + (t0 + t1)
        conv_back[pl.ds(3, Q, stride=4), :] = qb + (t0 + t2)
        for r in range(UTT_LEN // R):
            rows = pl.ds(pl.multiple_of(rows_u + r * R, R), R)
            acc = jnp.where(valid[r * R:(r + 1) * R], conv_back[r * R:(r + 1) * R, :], 0.0)
            value, gate = glu[rows, pl.ds(at, TILE)], glu[rows, pl.ds(at + TILE, TILE)]
            sig = jax.nn.sigmoid(gate)
            d_value = acc * sig
            d_gate = d_value * value * (1.0 - sig)
            to = pl.multiple_of(cb * 256, 256)
            dproj[rows, pl.ds(to, TILE)] = d_value.astype(BF16)
            dproj[rows, pl.ds(to + TILE, TILE)] = d_gate.astype(BF16)

    def channels(pair, c):
        columns = pl.ds(pl.multiple_of(pair * 512, 512), 512)
        for t in range(2):
            for part in range(2):
                load_weight(pair * 2 + t, part).wait()
        glu[...] = jnp.dot(frames_v[...], weight_v[:, columns], preferred_element_type=F32)

        def one(t, c):
            coefficients(pair * 2 + t)

            def utterance(u, c):
                conv_tile(u, pair * 2 + t, pl.multiple_of(t * 256, 256))
                hook(pair * 8 + t * 4 + u)
                return c

            return lax.fori_loop(0, 4, utterance, c)

        return lax.fori_loop(0, 2, one, c)

    lax.fori_loop(0, 4, channels, 0)

    def quarter(i):
        rows = pl.ds(pl.multiple_of(i % 2 * 512, 512), 512)
        return rows, pl.ds(pl.multiple_of(i // 2 * 512, 512), 512)

    def store(i):
        part = quarter(i)
        return pltpu.make_async_copy(out_v.at[*part], out.at[*part], store_sem.at[i])

    def back(i, c):
        rows, columns = quarter(i)
        out_v[rows, columns] = lax.dot_general(
            dproj[rows, :], weight_v[columns, :], (((1,), (1,)), ((), ())), preferred_element_type=F32
        ).astype(BF16)
        store(i).start()
        hook(32 + i)
        return c

    lax.fori_loop(0, 4, back, 0)

    for chunk in range(CHUNKS):
        each(16, lambda o: copy4(chunk, o).wait_recv())
    for chunk in range(CHUNKS):
        if chunk:
            each(16, lambda o: copy1(chunk, o).wait_send())
        copy2(chunk).wait_send()
        each(8, lambda o: copy3(chunk, o).wait_send())
        each(16, lambda o: copy4(chunk, o).wait_send())
    for i in range(4):
        store(i).wait()
    for chunk in range(CHUNKS):
        keep_own(chunk).wait()


def finish(owners_hbm, grad, gathered, out, owned, owners, through, blocks, owned_v, owners_sem, move_sem, block_sem, owned_sem):
    node = lax.axis_index("node")

    def move_in(i):
        rows = pl.ds(i * 256, 256)
        return pltpu.make_async_copy(grad.at[rows], through.at[rows], move_sem.at[0, i])

    def move_out(i):
        rows = pl.ds(i * 256, 256)
        return pltpu.make_async_copy(through.at[rows], out.at[rows], move_sem.at[1, i])

    load_owners = pltpu.make_async_copy(owners_hbm, owners, owners_sem)
    load_owners.start()
    for i in range(4):
        move_in(i).start()
    load_owners.wait()
    picks = [jnp.int32(-1)] * CAP
    held = jnp.int32(0)
    for i in range(32):
        mine = owners[i] == node
        picks = [jnp.where(mine & (held == k), i, picks[k]) for k in range(CAP)]
        held = held + mine.astype(I32)

    def fetch(k, g):
        block = jnp.maximum(picks[k], 0)
        return pltpu.make_async_copy(
            gathered.at[g * 8 + block // 4, block % 4], blocks.at[k, g], block_sem.at[k, g]
        )

    for k in range(CAP):
        for g in range(2):
            fetch(k, g).start()
    for i in range(4):
        move_in(i).wait()
        move_out(i).start()
    for k in range(CAP):
        keep = jnp.broadcast_to(picks[k] >= 0, (32, TILE))
        for g in range(2):
            fetch(k, g).wait()
            owned_v[k, g * 32:(g + 1) * 32, :] = jnp.where(keep, blocks[k, g].astype(F32), 0.0)
    last = pltpu.make_async_copy(owned_v, owned, owned_sem)
    last.start()
    for i in range(4):
        move_out(i).wait()
    last.wait()


SLOTS = (16, 22, 19, 26, 29, 33, 13)


def shards(frames, lengths, routes, owners, pw_weight, dw_kernel, conv_grad, hidden_grad):
    hbm = pl.BlockSpec(memory_space=pl.ANY)
    dma = pltpu.SemaphoreType.DMA
    grad, gathered = pl.pallas_call(
        functools.partial(kernel, SLOTS),
        out_shape=(
            jax.ShapeDtypeStruct((1024, 1024), BF16),
            jax.ShapeDtypeStruct((16, 4, 32, TILE), BF16),
        ),
        in_specs=[hbm] * 7,
        out_specs=(hbm, hbm),
        scratch_shapes=[
            pltpu.SMEM((1, 4), I32),
            pltpu.VMEM((2, 1024), I32),
            pltpu.VMEM((1024, 1024), BF16),
            pltpu.VMEM((CAPR, 4096), BF16),
            pltpu.VMEM((1024, 2048), BF16),
            pltpu.VMEM((KW, 1024), BF16),
            pltpu.VMEM((1024, 1024), BF16),
            pltpu.VMEM((1024, 1024), BF16),
            pltpu.VMEM((8, TILE), F32),
            pltpu.VMEM((1024, 512), F32),
            pltpu.VMEM((304, TILE), F32),
            pltpu.VMEM((40, TILE), F32),
            pltpu.VMEM((72, TILE), F32),
            pltpu.VMEM((9, 72, TILE), F32),
            pltpu.VMEM((256, TILE), F32),
            pltpu.VMEM((1024, 2048), BF16),
            pltpu.VMEM((16, 192, TILE), BF16),
            pltpu.VMEM((16, 192, TILE), BF16),
            pltpu.VMEM((CHUNKS, 2, 256, 256), F32),
            pltpu.VMEM((CHUNKS, 2, 256, 256), BF16),
            pltpu.VMEM((CHUNKS, 256, 256), BF16),
            pltpu.VMEM((CHUNKS, 8, 32, 256), BF16),
            pltpu.VMEM((CHUNKS, 8, 32, 256), BF16),
            pltpu.VMEM((CHUNKS, 2, 32, TILE), BF16),
            dma((22,)), dma((4,)),
            dma((CHUNKS, 16)), dma((CHUNKS, 16)),
            dma((CHUNKS,)), dma((CHUNKS,)),
            dma((CHUNKS, 8)), dma((CHUNKS, 8)),
            dma((CHUNKS, 16)), dma((CHUNKS, 16)),
        ],
        compiler_params=pltpu.CompilerParams(
            collective_id=0, has_side_effects=True, vmem_limit_bytes=56 * 2**20
        ),
    )(
        lengths, routes.T, frames, hidden_grad, pw_weight, dw_kernel, conv_grad
    )
    return pl.pallas_call(
        finish,
        out_shape=(
            jax.ShapeDtypeStruct((1024, 1024), BF16),
            jax.ShapeDtypeStruct((CAP, 64, TILE), F32),
        ),
        in_specs=[hbm] * 3,
        out_specs=(hbm, hbm),
        scratch_shapes=[
            pltpu.SMEM((32,), I32),
            pltpu.VMEM((1024, 1024), BF16),
            pltpu.VMEM((CAP, 2, 32, TILE), BF16),
            pltpu.VMEM((CAP, 64, TILE), F32),
            dma, dma((2, 4)), dma((CAP, 2)), dma,
        ],
        compiler_params=pltpu.CompilerParams(vmem_limit_bytes=56 * 2**20),
    )(owners.reshape(32), grad, gathered)


def solution(mesh):
    in_specs = (
        P(("node", "local"), None),
        P(("node", "local"), None),
        P(("node", "local"), None),
        P(),
        P(),
        P(),
        P(("node", "local"), None),
        P(("node", "local"), None, None),
    )
    out_specs = (P(("node", "local"), None), P("node", "local", None))
    return jax.shard_map(shards, mesh=mesh, in_specs=in_specs, out_specs=out_specs, check_vma=False)
```

```python
import functools

import jax
import jax.numpy as jnp
from jax import lax
from jax.experimental import pallas as pl
from jax.experimental.pallas import tpu as pltpu
from jax.sharding import PartitionSpec as P

MESH = pl.DeviceIdType.MESH
F32, BF16, I32 = jnp.float32, jnp.bfloat16, jnp.int32

TILE = 128
UTT_LEN = 256
KW = 31
FAR_FIRST = sorted(range(1, 16), key=lambda o: -min(o // 4, 4 - o // 4) - min(o % 4, 4 - o % 4))
CAPR = 24
CHUNKS = 2
CAP = 6


def kernel(
    slots,
    lengths_hbm, routes_hbm, frames, hidden, weight, taps_hbm, conv_grad,
    out, gathered,
    lengths, routes, frames_v, hidden_v, weight_v, taps_v, conv_v, out_v,
    flags, glu, padded, taps_f, coef, phase, conv_back, dproj,
    send1, recv1, piece, piece_b, recv2, half_b, recv3, total_b,
    load_sem, store_sem,
    send1_sem, recv1_sem, send2_sem, recv2_sem, send3_sem, recv3_sem, send4_sem, recv4_sem,
):
    node, local = lax.axis_index("node"), lax.axis_index("local")
    z, core = local // 2, local % 2
    partner = local + 1 - 2 * core
    y, x = node // 4, node % 4

    def load(source, target, i):
        return pltpu.make_async_copy(source, target, load_sem.at[i])

    def load_weight(cb, part):
        start = pl.multiple_of(cb * TILE, TILE)
        return load(
            weight.at[:, pl.ds(part * 1024 + start, TILE)],
            weight_v.at[:, pl.ds(pl.multiple_of(cb * 256, 256) + part * TILE, TILE)],
            4 + cb * 2 + part,
        )

    load_frames = load(frames, frames_v, 0)
    load_hidden = load(hidden.at[0], hidden_v, 1)
    load_taps = load(taps_hbm, taps_v, 2)
    load_conv = load(conv_grad, conv_v, 3)
    load_lengths = load(lengths_hbm, lengths, 20)
    load_routes = load(routes_hbm, routes, 21)
    load_routes.start()
    load_lengths.start()
    load_frames.start()
    load_hidden.start()
    load_weight(0, 0).start()
    load_weight(0, 1).start()
    load_weight(1, 0).start()
    load_weight(1, 1).start()
    load_taps.start()
    load_conv.start()

    barrier = pltpu.get_barrier_semaphore()

    def greet(o, c):
        pl.semaphore_signal(barrier, inc=1, device_id=((node + o) % 16, local), device_id_type=MESH)
        return c

    def greet_z(o, c):
        pl.semaphore_signal(
            barrier, inc=1, device_id=(node, (z + o) % 8 * 2 + core), device_id_type=MESH
        )
        return c

    lax.fori_loop(1, 16, greet, 0)
    lax.fori_loop(1, 8, greet_z, 0)
    pl.semaphore_signal(barrier, inc=1, device_id=(node, partner), device_id_type=MESH)

    load_routes.wait()
    load_lengths.wait()
    lane = lax.broadcasted_iota(I32, (1, TILE), 1)
    for r in range(8):
        named = routes[:, r * TILE:(r + 1) * TILE] == 0
        named = jnp.max(named.astype(I32), axis=0, keepdims=True)
        valid = lane + (r % 2) * TILE < lengths[0, r // 2]
        flags[r:r + 1, :] = jnp.where(valid, named, 0).astype(F32)
    routed = flags[...]
    upto = (
        lax.broadcasted_iota(I32, (TILE, TILE), 0) <= lax.broadcasted_iota(I32, (TILE, TILE), 1)
    ).astype(F32)
    before = (
        lax.broadcasted_iota(I32, (8, 8), 1) < lax.broadcasted_iota(I32, (8, 8), 0)
    ).astype(F32)
    in_row = jnp.dot(routed, upto, preferred_element_type=F32)
    row_sum = jnp.broadcast_to(jnp.sum(routed, axis=1, keepdims=True), (8, TILE))
    order = in_row + jnp.dot(before, row_sum, preferred_element_type=F32)
    flags[...] = jnp.where(routed > 0, order - 1.0, -1.0)
    want = lax.broadcasted_iota(I32, (32, TILE), 0).astype(F32)
    chosen = jnp.concatenate(
        [(jnp.broadcast_to(flags[r:r + 1, :], (32, TILE)) == want).astype(F32) for r in range(8)], axis=1
    ).astype(BF16)
    load_frames.wait()
    slot = jnp.dot(chosen, frames_v[...], preferred_element_type=F32)[0:CAPR]

    group = lax.broadcasted_iota(I32, (CAPR, TILE), 1) // 32
    sets = []
    for g in range(2):
        tiles = []
        for c in range(2):
            for half in range(2):
                tile = None
                for i in range(4):
                    zz = half * 4 + i
                    part = pltpu.roll(slot[:, zz * TILE:(zz + 1) * TILE], ((i - (2 * c + g)) * 32) % TILE, 1)
                    tile = part if tile is None else jnp.where(group == i, part, tile)
                tiles.append(tile)
        sets.append(jnp.concatenate(tiles, axis=0).astype(BF16))
    load_hidden.wait()
    for m in range(8):
        columns = [
            hidden_v[:, (m * 4 + t) * TILE:(m * 4 + t + 1) * TILE].astype(F32) for t in range(4)
        ]
        columns = jnp.concatenate(columns, axis=0).astype(BF16)
        for g in range(2):
            send1[g * 8 + m, 0:96, :] = sets[g]
            send1[g * 8 + m, 96:192, :] = columns
    recv1[node] = send1[node]

    pl.semaphore_wait(barrier, 23)

    rows1 = ((0, 144), (144, 48))

    def copy1(chunk, o):
        to = (y + o // 4) % 4 * 4 + (x + o % 4) % 4
        rows = pl.ds(*rows1[chunk])
        return pltpu.make_async_remote_copy(
            src_ref=send1.at[to, rows], dst_ref=recv1.at[node, rows],
            send_sem=send1_sem.at[chunk, o], recv_sem=recv1_sem.at[chunk, o],
            device_id=(to, local), device_id_type=MESH,
        )

    def copy2(chunk):
        return pltpu.make_async_remote_copy(
            src_ref=piece_b.at[chunk, 1 - core], dst_ref=recv2.at[chunk],
            send_sem=send2_sem.at[chunk], recv_sem=recv2_sem.at[chunk],
            device_id=(node, partner), device_id_type=MESH,
        )

    def copy3(chunk, o):
        to = (z + o) % 8
        return pltpu.make_async_remote_copy(
            src_ref=half_b.at[chunk, to], dst_ref=recv3.at[chunk, z],
            send_sem=send3_sem.at[chunk, o], recv_sem=recv3_sem.at[chunk, o],
            device_id=(node, to * 2 + core), device_id_type=MESH,
        )

    def copy4(chunk, o):
        to = (y + o // 4) % 4 * 4 + (x + o % 4) % 4
        return pltpu.make_async_remote_copy(
            src_ref=total_b.at[chunk], dst_ref=gathered.at[node, pl.ds(2 * chunk, 2)],
            send_sem=send4_sem.at[chunk, o], recv_sem=recv4_sem.at[chunk, o],
            device_id=(to, local), device_id_type=MESH,
        )

    def keep_own(chunk):
        return pltpu.make_async_copy(
            total_b.at[chunk], gathered.at[node, pl.ds(2 * chunk, 2)], load_sem.at[chunk]
        )

    def each(count, do):
        def step(o, c):
            do(o)
            return c

        lax.fori_loop(1, count, step, 0)

    for o in FAR_FIRST:
        copy1(0, o).start()
    for cb in range(2, 8):
        load_weight(cb, 0).start()
        load_weight(cb, 1).start()


    def send_rest():
        each(16, lambda o: copy1(0, o).wait_send())
        for o in FAR_FIRST:
            copy1(1, o).start()

    def multiply(chunk):
        each(16, lambda o: copy1(chunk, o).wait_recv())

        def tiles(first, count):
            rows = recv1[:, first * CAPR:(first + count) * CAPR, :].astype(F32)
            rows = rows.reshape(16, count, CAPR, TILE)
            parts = [rows[:, t].reshape(16 * CAPR, TILE) for t in range(count)]
            return jnp.concatenate(parts, axis=1).astype(BF16)

        left, right = tiles(0, 4), tiles(4 + 2 * chunk, 2)
        both = lax.dot_general(left, right, (((0,), (0,)), ((), ())), preferred_element_type=F32)
        both = both.reshape(2, 256, 256)
        piece[chunk] = both
        piece_b[chunk] = both.astype(BF16)
        copy2(chunk).start()

    def add_cores(chunk):
        copy2(chunk).wait_recv()
        half = piece[chunk, core] + recv2[chunk].astype(F32)
        half_b[chunk] = half.astype(BF16).reshape(8, 32, 256)
        recv3[chunk, z] = half_b[chunk, z]
        for o in (4, 3, 5, 2, 6, 1, 7):
            copy3(chunk, o).start()

    def add_chips(chunk):
        each(8, lambda o: copy3(chunk, o).wait_recv())
        total = recv3[chunk, 0].astype(F32)
        for other in range(1, 8):
            total = total + recv3[chunk, other].astype(F32)
        total = total.astype(BF16)
        for t in range(2):
            total_b[chunk, t] = total[:, t * TILE:(t + 1) * TILE]
        keep_own(chunk).start()
        for o in FAR_FIRST:
            copy4(chunk, o).start()

    steps = {
        slots[6]: send_rest,
        slots[0]: lambda: multiply(0),
        slots[1]: lambda: multiply(1),
        slots[2]: lambda: add_cores(0),
        slots[3]: lambda: add_cores(1),
        slots[4]: lambda: add_chips(0),
        slots[5]: lambda: add_chips(1),
    }

    def hook(now):
        for at, step in steps.items():
            pl.when(now == at)(step)

    padded[0:16, :] = jnp.zeros((16, TILE), F32)
    padded[272:304, :] = jnp.zeros((32, TILE), F32)
    taps_f[...] = jnp.zeros((40, TILE), F32)
    load_taps.wait()
    load_conv.wait()
    R = 64
    Q = UTT_LEN // 4

    def coefficients(cb):
        taps_f[1:KW + 1, :] = taps_v[:, pl.ds(pl.multiple_of(cb * TILE, TILE), TILE)].astype(F32)
        u0, u1, u2, u3 = (taps_f[pl.ds(3 - m, 8, stride=4), :] for m in range(4))
        filters = (u0 + u1 + u2 + u3, u0 + u1, u2 + u3, u0 + u2, u0, u2, u1 + u3, u1, u3)
        for i, rows in enumerate(filters):
            coef[i * 8:i * 8 + 8, :] = rows

    def conv_tile(u, cb, at):
        rows_u = pl.multiple_of(u * UTT_LEN, UTT_LEN)
        lanes = pl.ds(pl.multiple_of(cb * TILE, TILE), TILE)
        valid = lax.broadcasted_iota(I32, (UTT_LEN, TILE), 0) < lengths[0, u]
        padded[16:272, :] = jnp.where(valid, conv_v[pl.ds(rows_u, UTT_LEN), lanes].astype(F32), 0.0)
        x0, x1, x2, x3, x4, x5, x6 = (padded[pl.ds(1 + m, Q + 8, stride=4), :] for m in range(7))
        d0, d1, d2 = x0 - x1, x2 - x3, x4 - x5
        e0, e1, e2 = x2 - x1, x4 - x3, x6 - x5
        inputs = (x3, x1 - x3, x5 - x3, d1, d0 - d1, d2 - d1, e1, e0 - e1, e2 - e1)
        for i, rows in enumerate(inputs):
            phase[i] = rows

        def correlate(i):
            acc = None
            for j in range(8):
                term = coef[i * 8 + 7 - j:i * 8 + 8 - j, :] * phase[i, j:j + Q, :]
                acc = term if acc is None else acc + term
            return acc

        q0, q1, q2 = correlate(0), correlate(1), correlate(2)
        qa, qb = q0 + q1, q0 + q2
        r0, r1, r2 = correlate(3), correlate(4), correlate(5)
        conv_back[pl.ds(0, Q, stride=4), :] = qa + (r0 + r1)
        conv_back[pl.ds(2, Q, stride=4), :] = qb + (r0 + r2)
        t0, t1, t2 = correlate(6), correlate(7), correlate(8)
        conv_back[pl.ds(1, Q, stride=4), :] = qa + (t0 + t1)
        conv_back[pl.ds(3, Q, stride=4), :] = qb + (t0 + t2)
        for r in range(UTT_LEN // R):
            rows = pl.ds(pl.multiple_of(rows_u + r * R, R), R)
            acc = jnp.where(valid[r * R:(r + 1) * R], conv_back[r * R:(r + 1) * R, :], 0.0)
            value, gate = glu[rows, pl.ds(at, TILE)], glu[rows, pl.ds(at + TILE, TILE)]
            sig = jax.nn.sigmoid(gate)
            d_value = acc * sig
            d_gate = d_value * value * (1.0 - sig)
            to = pl.multiple_of(cb * 256, 256)
            dproj[rows, pl.ds(to, TILE)] = d_value.astype(BF16)
            dproj[rows, pl.ds(to + TILE, TILE)] = d_gate.astype(BF16)

    def channels(pair, c):
        columns = pl.ds(pl.multiple_of(pair * 512, 512), 512)
        for t in range(2):
            for part in range(2):
                load_weight(pair * 2 + t, part).wait()
        glu[...] = jnp.dot(frames_v[...], weight_v[:, columns], preferred_element_type=F32)

        def one(t, c):
            coefficients(pair * 2 + t)

            def utterance(u, c):
                conv_tile(u, pair * 2 + t, pl.multiple_of(t * 256, 256))
                hook(pair * 8 + t * 4 + u)
                return c

            return lax.fori_loop(0, 4, utterance, c)

        return lax.fori_loop(0, 2, one, c)

    lax.fori_loop(0, 4, channels, 0)

    def quarter(i):
        rows = pl.ds(pl.multiple_of(i % 2 * 512, 512), 512)
        return rows, pl.ds(pl.multiple_of(i // 2 * 512, 512), 512)

    def store(i):
        part = quarter(i)
        return pltpu.make_async_copy(out_v.at[*part], out.at[*part], store_sem.at[i])

    def back(i, c):
        rows, columns = quarter(i)
        out_v[rows, columns] = lax.dot_general(
            dproj[rows, :], weight_v[columns, :], (((1,), (1,)), ((), ())), preferred_element_type=F32
        ).astype(BF16)
        store(i).start()
        hook(32 + i)
        return c

    lax.fori_loop(0, 4, back, 0)

    for chunk in range(CHUNKS):
        each(16, lambda o: copy4(chunk, o).wait_recv())
    for chunk in range(CHUNKS):
        if chunk:
            each(16, lambda o: copy1(chunk, o).wait_send())
        copy2(chunk).wait_send()
        each(8, lambda o: copy3(chunk, o).wait_send())
        each(16, lambda o: copy4(chunk, o).wait_send())
    for i in range(4):
        store(i).wait()
    for chunk in range(CHUNKS):
        keep_own(chunk).wait()


def finish(owners_hbm, grad, gathered, out, owned, owners, through, blocks, owned_v, owners_sem, move_sem, block_sem, owned_sem):
    node = lax.axis_index("node")

    def move_in(i):
        rows = pl.ds(i * 256, 256)
        return pltpu.make_async_copy(grad.at[rows], through.at[rows], move_sem.at[0, i])

    def move_out(i):
        rows = pl.ds(i * 256, 256)
        return pltpu.make_async_copy(through.at[rows], out.at[rows], move_sem.at[1, i])

    load_owners = pltpu.make_async_copy(owners_hbm, owners, owners_sem)
    load_owners.start()
    for i in range(4):
        move_in(i).start()
    load_owners.wait()
    picks = [jnp.int32(-1)] * CAP
    held = jnp.int32(0)
    for i in range(32):
        mine = owners[i] == node
        picks = [jnp.where(mine & (held == k), i, picks[k]) for k in range(CAP)]
        held = held + mine.astype(I32)

    def fetch(k, g):
        block = jnp.maximum(picks[k], 0)
        return pltpu.make_async_copy(
            gathered.at[g * 8 + block // 4, block % 4], blocks.at[k, g], block_sem.at[k, g]
        )

    for k in range(CAP):
        for g in range(2):
            fetch(k, g).start()
    for i in range(4):
        move_in(i).wait()
        move_out(i).start()
    for k in range(CAP):
        keep = jnp.broadcast_to(picks[k] >= 0, (32, TILE))
        for g in range(2):
            fetch(k, g).wait()
            owned_v[k, g * 32:(g + 1) * 32, :] = jnp.where(keep, blocks[k, g].astype(F32), 0.0)
    last = pltpu.make_async_copy(owned_v, owned, owned_sem)
    last.start()
    for i in range(4):
        move_out(i).wait()
    last.wait()


SLOTS = (16, 22, 19, 26, 29, 33, 13)


def shards(frames, lengths, routes, owners, pw_weight, dw_kernel, conv_grad, hidden_grad):
    hbm = pl.BlockSpec(memory_space=pl.ANY)
    dma = pltpu.SemaphoreType.DMA
    grad, gathered = pl.pallas_call(
        functools.partial(kernel, SLOTS),
        out_shape=(
            jax.ShapeDtypeStruct((1024, 1024), BF16),
            jax.ShapeDtypeStruct((16, 4, 32, TILE), BF16),
        ),
        in_specs=[hbm] * 7,
        out_specs=(hbm, hbm),
        scratch_shapes=[
            pltpu.SMEM((1, 4), I32),
            pltpu.VMEM((2, 1024), I32),
            pltpu.VMEM((1024, 1024), BF16),
            pltpu.VMEM((CAPR, 4096), BF16),
            pltpu.VMEM((1024, 2048), BF16),
            pltpu.VMEM((KW, 1024), BF16),
            pltpu.VMEM((1024, 1024), BF16),
            pltpu.VMEM((1024, 1024), BF16),
            pltpu.VMEM((8, TILE), F32),
            pltpu.VMEM((1024, 512), F32),
            pltpu.VMEM((304, TILE), F32),
            pltpu.VMEM((40, TILE), F32),
            pltpu.VMEM((72, TILE), F32),
            pltpu.VMEM((9, 72, TILE), F32),
            pltpu.VMEM((256, TILE), F32),
            pltpu.VMEM((1024, 2048), BF16),
            pltpu.VMEM((16, 192, TILE), BF16),
            pltpu.VMEM((16, 192, TILE), BF16),
            pltpu.VMEM((CHUNKS, 2, 256, 256), F32),
            pltpu.VMEM((CHUNKS, 2, 256, 256), BF16),
            pltpu.VMEM((CHUNKS, 256, 256), BF16),
            pltpu.VMEM((CHUNKS, 8, 32, 256), BF16),
            pltpu.VMEM((CHUNKS, 8, 32, 256), BF16),
            pltpu.VMEM((CHUNKS, 2, 32, TILE), BF16),
            dma((22,)), dma((4,)),
            dma((CHUNKS, 16)), dma((CHUNKS, 16)),
            dma((CHUNKS,)), dma((CHUNKS,)),
            dma((CHUNKS, 8)), dma((CHUNKS, 8)),
            dma((CHUNKS, 16)), dma((CHUNKS, 16)),
        ],
        compiler_params=pltpu.CompilerParams(
            collective_id=0, has_side_effects=True, vmem_limit_bytes=56 * 2**20
        ),
    )(
        lengths, routes.T, frames, hidden_grad, pw_weight, dw_kernel, conv_grad
    )
    return pl.pallas_call(
        finish,
        out_shape=(
            jax.ShapeDtypeStruct((1024, 1024), BF16),
            jax.ShapeDtypeStruct((CAP, 64, TILE), F32),
        ),
        in_specs=[hbm] * 3,
        out_specs=(hbm, hbm),
        scratch_shapes=[
            pltpu.SMEM((32,), I32),
            pltpu.VMEM((1024, 1024), BF16),
            pltpu.VMEM((CAP, 2, 32, TILE), BF16),
            pltpu.VMEM((CAP, 64, TILE), F32),
            dma, dma((2, 4)), dma((CAP, 2)), dma,
        ],
        compiler_params=pltpu.CompilerParams(vmem_limit_bytes=56 * 2**20),
    )(owners.reshape(32), grad, gathered)


def solution(mesh):
    in_specs = (
        P(("node", "local"), None),
        P(("node", "local"), None),
        P(("node", "local"), None),
        P(),
        P(),
        P(),
        P(("node", "local"), None),
        P(("node", "local"), None, None),
    )
    out_specs = (P(("node", "local"), None), P("node", "local", None))
    return jax.shard_map(shards, mesh=mesh, in_specs=in_specs, out_specs=out_specs, check_vma=False)
```

```python
import functools

import jax
import jax.numpy as jnp
from jax import lax
from jax.experimental import pallas as pl
from jax.experimental.pallas import tpu as pltpu
from jax.sharding import PartitionSpec as P

MESH = pl.DeviceIdType.MESH
F32, BF16, I32 = jnp.float32, jnp.bfloat16, jnp.int32

TILE = 128
UTT_LEN = 256
KW = 31
FAR_FIRST = sorted(range(1, 16), key=lambda o: -min(o // 4, 4 - o // 4) - min(o % 4, 4 - o % 4))
CAPR = 24
CHUNKS = 2
CAP = 6


def kernel(
    slots,
    lengths_hbm, routes_hbm, frames, hidden, weight, taps_hbm, conv_grad,
    out, gathered,
    lengths, routes, frames_v, hidden_v, weight_v, taps_v, conv_v, out_v,
    flags, glu, padded, taps_f, coef, phase, conv_back, dproj,
    send1, recv1, left_t, piece, piece_b, recv2, half_b, recv3, total_b,
    load_sem, store_sem,
    send1_sem, recv1_sem, send2_sem, recv2_sem, send3_sem, recv3_sem, send4_sem, recv4_sem,
):
    node, local = lax.axis_index("node"), lax.axis_index("local")
    z, core = local // 2, local % 2
    partner = local + 1 - 2 * core
    y, x = node // 4, node % 4

    def load(source, target, i):
        return pltpu.make_async_copy(source, target, load_sem.at[i])

    def load_weight(cb, part):
        start = pl.multiple_of(cb * TILE, TILE)
        return load(
            weight.at[:, pl.ds(part * 1024 + start, TILE)],
            weight_v.at[:, pl.ds(pl.multiple_of(cb * 256, 256) + part * TILE, TILE)],
            4 + cb * 2 + part,
        )

    load_frames = load(frames, frames_v, 0)
    load_hidden = load(hidden.at[0], hidden_v, 1)
    load_taps = load(taps_hbm, taps_v, 2)
    load_conv = load(conv_grad, conv_v, 3)
    load_lengths = load(lengths_hbm, lengths, 20)
    load_routes = load(routes_hbm, routes, 21)
    load_routes.start()
    load_lengths.start()
    load_frames.start()
    load_hidden.start()
    load_weight(0, 0).start()
    load_weight(0, 1).start()
    load_weight(1, 0).start()
    load_weight(1, 1).start()
    load_taps.start()
    load_conv.start()

    barrier = pltpu.get_barrier_semaphore()

    def greet(o, c):
        pl.semaphore_signal(barrier, inc=1, device_id=((node + o) % 16, local), device_id_type=MESH)
        return c

    def greet_z(o, c):
        pl.semaphore_signal(
            barrier, inc=1, device_id=(node, (z + o) % 8 * 2 + core), device_id_type=MESH
        )
        return c

    lax.fori_loop(1, 16, greet, 0)
    lax.fori_loop(1, 8, greet_z, 0)
    pl.semaphore_signal(barrier, inc=1, device_id=(node, partner), device_id_type=MESH)

    load_routes.wait()
    load_lengths.wait()
    lane = lax.broadcasted_iota(I32, (1, TILE), 1)
    for r in range(8):
        named = routes[:, r * TILE:(r + 1) * TILE] == 0
        named = jnp.max(named.astype(I32), axis=0, keepdims=True)
        valid = lane + (r % 2) * TILE < lengths[0, r // 2]
        flags[r:r + 1, :] = jnp.where(valid, named, 0).astype(F32)
    routed = flags[...]
    upto = (
        lax.broadcasted_iota(I32, (TILE, TILE), 0) <= lax.broadcasted_iota(I32, (TILE, TILE), 1)
    ).astype(F32)
    before = (
        lax.broadcasted_iota(I32, (8, 8), 1) < lax.broadcasted_iota(I32, (8, 8), 0)
    ).astype(F32)
    in_row = jnp.dot(routed, upto, preferred_element_type=F32)
    row_sum = jnp.broadcast_to(jnp.sum(routed, axis=1, keepdims=True), (8, TILE))
    order = in_row + jnp.dot(before, row_sum, preferred_element_type=F32)
    flags[...] = jnp.where(routed > 0, order - 1.0, -1.0)
    want = lax.broadcasted_iota(I32, (32, TILE), 0).astype(F32)
    chosen = jnp.concatenate(
        [(jnp.broadcast_to(flags[r:r + 1, :], (32, TILE)) == want).astype(F32) for r in range(8)], axis=1
    ).astype(BF16)
    load_frames.wait()
    slot = jnp.dot(chosen, frames_v[...], preferred_element_type=F32)[0:CAPR]

    group = lax.broadcasted_iota(I32, (CAPR, TILE), 1) // 32
    sets = []
    for g in range(2):
        tiles = []
        for c in range(2):
            for half in range(2):
                tile = None
                for i in range(4):
                    zz = half * 4 + i
                    part = pltpu.roll(slot[:, zz * TILE:(zz + 1) * TILE], ((i - (2 * c + g)) * 32) % TILE, 1)
                    tile = part if tile is None else jnp.where(group == i, part, tile)
                tiles.append(tile)
        sets.append(jnp.concatenate(tiles, axis=0).astype(BF16))
    load_hidden.wait()
    for m in range(8):
        columns = [
            hidden_v[:, (m * 4 + t) * TILE:(m * 4 + t + 1) * TILE].astype(F32) for t in range(4)
        ]
        columns = jnp.concatenate(columns, axis=0).astype(BF16)
        for g in range(2):
            send1[g * 8 + m, 0:96, :] = sets[g]
            send1[g * 8 + m, 96:192, :] = columns
    recv1[node] = send1[node]

    pl.semaphore_wait(barrier, 23)

    rows1 = ((0, 144), (144, 48))

    def copy1(chunk, o):
        to = (y + o // 4) % 4 * 4 + (x + o % 4) % 4
        rows = pl.ds(*rows1[chunk])
        return pltpu.make_async_remote_copy(
            src_ref=send1.at[to, rows], dst_ref=recv1.at[node, rows],
            send_sem=send1_sem.at[chunk, o], recv_sem=recv1_sem.at[chunk, o],
            device_id=(to, local), device_id_type=MESH,
        )

    def copy2(chunk):
        return pltpu.make_async_remote_copy(
            src_ref=piece_b.at[chunk, 1 - core], dst_ref=recv2.at[chunk],
            send_sem=send2_sem.at[chunk], recv_sem=recv2_sem.at[chunk],
            device_id=(node, partner), device_id_type=MESH,
        )

    def copy3(chunk, o):
        to = (z + o) % 8
        return pltpu.make_async_remote_copy(
            src_ref=half_b.at[chunk, to], dst_ref=recv3.at[chunk, z],
            send_sem=send3_sem.at[chunk, o], recv_sem=recv3_sem.at[chunk, o],
            device_id=(node, to * 2 + core), device_id_type=MESH,
        )

    def copy4(chunk, o):
        to = (y + o // 4) % 4 * 4 + (x + o % 4) % 4
        return pltpu.make_async_remote_copy(
            src_ref=total_b.at[chunk], dst_ref=gathered.at[node, pl.ds(2 * chunk, 2)],
            send_sem=send4_sem.at[chunk, o], recv_sem=recv4_sem.at[chunk, o],
            device_id=(to, local), device_id_type=MESH,
        )

    def keep_own(chunk):
        return pltpu.make_async_copy(
            total_b.at[chunk], gathered.at[node, pl.ds(2 * chunk, 2)], load_sem.at[chunk]
        )

    def each(count, do):
        def step(o, c):
            do(o)
            return c

        lax.fori_loop(1, count, step, 0)

    for o in FAR_FIRST:
        copy1(0, o).start()
    for cb in range(2, 8):
        load_weight(cb, 0).start()
        load_weight(cb, 1).start()


    def send_rest():
        each(16, lambda o: copy1(0, o).wait_send())
        for o in FAR_FIRST:
            copy1(1, o).start()

    def multiply(chunk):
        each(16, lambda o: copy1(chunk, o).wait_recv())

        def tiles(first, count):
            rows = recv1[:, first * CAPR:(first + count) * CAPR, :].astype(F32)
            rows = rows.reshape(16, count, CAPR, TILE)
            parts = [rows[:, t].reshape(16 * CAPR, TILE) for t in range(count)]
            return jnp.concatenate(parts, axis=1).astype(BF16)

        if chunk == 0:
            left_t[...] = tiles(0, 4).T
        both = jnp.dot(left_t[...], tiles(4 + 2 * chunk, 2), preferred_element_type=F32)
        both = both.reshape(2, 256, 256)
        piece[chunk] = both
        piece_b[chunk] = both.astype(BF16)
        copy2(chunk).start()

    def add_cores(chunk):
        copy2(chunk).wait_recv()
        half = piece[chunk, core] + recv2[chunk].astype(F32)
        half_b[chunk] = half.astype(BF16).reshape(8, 32, 256)
        recv3[chunk, z] = half_b[chunk, z]
        for o in (4, 3, 5, 2, 6, 1, 7):
            copy3(chunk, o).start()

    def add_chips(chunk):
        each(8, lambda o: copy3(chunk, o).wait_recv())
        total = recv3[chunk, 0].astype(F32)
        for other in range(1, 8):
            total = total + recv3[chunk, other].astype(F32)
        total = total.astype(BF16)
        for t in range(2):
            total_b[chunk, t] = total[:, t * TILE:(t + 1) * TILE]
        for o in FAR_FIRST:
            copy4(chunk, o).start()
        keep_own(chunk).start()

    steps = {
        slots[6]: send_rest,
        slots[0]: lambda: multiply(0),
        slots[1]: lambda: multiply(1),
        slots[2]: lambda: add_cores(0),
        slots[3]: lambda: add_cores(1),
        slots[4]: lambda: add_chips(0),
        slots[5]: lambda: add_chips(1),
    }

    def hook(now):
        for at, step in steps.items():
            pl.when(now == at)(step)

    padded[0:16, :] = jnp.zeros((16, TILE), F32)
    padded[272:304, :] = jnp.zeros((32, TILE), F32)
    taps_f[...] = jnp.zeros((40, TILE), F32)
    load_taps.wait()
    load_conv.wait()
    R = 64
    Q = UTT_LEN // 4

    def coefficients(cb):
        taps_f[1:KW + 1, :] = taps_v[:, pl.ds(pl.multiple_of(cb * TILE, TILE), TILE)].astype(F32)
        u0, u1, u2, u3 = (taps_f[pl.ds(3 - m, 8, stride=4), :] for m in range(4))
        filters = (u0 + u1 + u2 + u3, u0 + u1, u2 + u3, u0 + u2, u0, u2, u1 + u3, u1, u3)
        for i, rows in enumerate(filters):
            coef[i * 8:i * 8 + 8, :] = rows

    def conv_tile(u, cb, at):
        rows_u = pl.multiple_of(u * UTT_LEN, UTT_LEN)
        lanes = pl.ds(pl.multiple_of(cb * TILE, TILE), TILE)
        valid = lax.broadcasted_iota(I32, (UTT_LEN, TILE), 0) < lengths[0, u]
        padded[16:272, :] = jnp.where(valid, conv_v[pl.ds(rows_u, UTT_LEN), lanes].astype(F32), 0.0)
        x0, x1, x2, x3, x4, x5, x6 = (padded[pl.ds(1 + m, Q + 8, stride=4), :] for m in range(7))
        d0, d1, d2 = x0 - x1, x2 - x3, x4 - x5
        e0, e1, e2 = x2 - x1, x4 - x3, x6 - x5
        inputs = (x3, x1 - x3, x5 - x3, d1, d0 - d1, d2 - d1, e1, e0 - e1, e2 - e1)
        for i, rows in enumerate(inputs):
            phase[i] = rows

        def correlate(i):
            acc = None
            for j in range(8):
                term = coef[i * 8 + 7 - j:i * 8 + 8 - j, :] * phase[i, j:j + Q, :]
                acc = term if acc is None else acc + term
            return acc

        q0, q1, q2 = correlate(0), correlate(1), correlate(2)
        qa, qb = q0 + q1, q0 + q2
        r0, r1, r2 = correlate(3), correlate(4), correlate(5)
        conv_back[pl.ds(0, Q, stride=4), :] = qa + (r0 + r1)
        conv_back[pl.ds(2, Q, stride=4), :] = qb + (r0 + r2)
        t0, t1, t2 = correlate(6), correlate(7), correlate(8)
        conv_back[pl.ds(1, Q, stride=4), :] = qa + (t0 + t1)
        conv_back[pl.ds(3, Q, stride=4), :] = qb + (t0 + t2)
        for r in range(UTT_LEN // R):
            rows = pl.ds(pl.multiple_of(rows_u + r * R, R), R)
            acc = jnp.where(valid[r * R:(r + 1) * R], conv_back[r * R:(r + 1) * R, :], 0.0)
            value, gate = glu[rows, pl.ds(at, TILE)], glu[rows, pl.ds(at + TILE, TILE)]
            sig = jax.nn.sigmoid(gate)
            d_value = acc * sig
            d_gate = d_value * value * (1.0 - sig)
            to = pl.multiple_of(cb * 256, 256)
            dproj[rows, pl.ds(to, TILE)] = d_value.astype(BF16)
            dproj[rows, pl.ds(to + TILE, TILE)] = d_gate.astype(BF16)

    def channels(pair, c):
        columns = pl.ds(pl.multiple_of(pair * 512, 512), 512)
        for t in range(2):
            for part in range(2):
                load_weight(pair * 2 + t, part).wait()
        glu[...] = jnp.dot(frames_v[...], weight_v[:, columns], preferred_element_type=F32)

        def one(t, c):
            coefficients(pair * 2 + t)

            def utterance(u, c):
                conv_tile(u, pair * 2 + t, pl.multiple_of(t * 256, 256))
                hook(pair * 8 + t * 4 + u)
                return c

            return lax.fori_loop(0, 4, utterance, c)

        return lax.fori_loop(0, 2, one, c)

    lax.fori_loop(0, 4, channels, 0)

    def quarter(i):
        rows = pl.ds(pl.multiple_of(i % 2 * 512, 512), 512)
        return rows, pl.ds(pl.multiple_of(i // 2 * 512, 512), 512)

    def store(i):
        part = quarter(i)
        return pltpu.make_async_copy(out_v.at[*part], out.at[*part], store_sem.at[i])

    def back(i, c):
        rows, columns = quarter(i)
        out_v[rows, columns] = lax.dot_general(
            dproj[rows, :], weight_v[columns, :], (((1,), (1,)), ((), ())), preferred_element_type=F32
        ).astype(BF16)
        store(i).start()
        hook(32 + i)
        return c

    lax.fori_loop(0, 4, back, 0)

    each(16, lambda o: copy1(1, o).wait_send())
    for chunk in range(CHUNKS):
        copy2(chunk).wait_send()
        each(8, lambda o: copy3(chunk, o).wait_send())
        keep_own(chunk).wait()
    for i in range(4):
        store(i).wait()
    for chunk in range(CHUNKS):
        each(16, lambda o: copy4(chunk, o).wait_send())
    for chunk in range(CHUNKS):
        each(16, lambda o: copy4(chunk, o).wait_recv())


def finish(owners_hbm, grad, gathered, out, owned, owners, picks, through, blocks, owned_v, owners_sem, move_sem, block_sem, owned_sem):
    node = lax.axis_index("node")

    def move_in(i):
        rows = pl.ds(i * 256, 256)
        return pltpu.make_async_copy(grad.at[rows], through.at[rows], move_sem.at[0, i])

    def move_out(i):
        rows = pl.ds(i * 256, 256)
        return pltpu.make_async_copy(through.at[rows], out.at[rows], move_sem.at[1, i])

    load_owners = pltpu.make_async_copy(owners_hbm, owners, owners_sem)
    load_owners.start()
    for i in range(4):
        move_in(i).start()
    load_owners.wait()
    held = jnp.int32(0)
    for i in range(32):
        picks[held] = jnp.int32(i)
        held = held + (owners[i] == node).astype(I32)

    def fetch(k, g):
        block = jnp.where(k < held, picks[k], 0)
        return pltpu.make_async_copy(
            gathered.at[g * 8 + block // 4, block % 4], blocks.at[k, g], block_sem.at[k, g]
        )

    for k in range(CAP):
        for g in range(2):
            fetch(k, g).start()
    for i in range(4):
        move_in(i).wait()
        move_out(i).start()
    for k in range(CAP):
        keep = jnp.broadcast_to(k < held, (32, TILE))
        for g in range(2):
            fetch(k, g).wait()
            owned_v[k, g * 32:(g + 1) * 32, :] = jnp.where(keep, blocks[k, g].astype(F32), 0.0)
    last = pltpu.make_async_copy(owned_v, owned, owned_sem)
    last.start()
    for i in range(4):
        move_out(i).wait()
    last.wait()


SLOTS = (16, 22, 19, 26, 29, 33, 13)


def shards(frames, lengths, routes, owners, pw_weight, dw_kernel, conv_grad, hidden_grad):
    hbm = pl.BlockSpec(memory_space=pl.ANY)
    dma = pltpu.SemaphoreType.DMA
    grad, gathered = pl.pallas_call(
        functools.partial(kernel, SLOTS),
        out_shape=(
            jax.ShapeDtypeStruct((1024, 1024), BF16),
            jax.ShapeDtypeStruct((16, 4, 32, TILE), BF16),
        ),
        in_specs=[hbm] * 7,
        out_specs=(hbm, hbm),
        scratch_shapes=[
            pltpu.SMEM((1, 4), I32),
            pltpu.VMEM((2, 1024), I32),
            pltpu.VMEM((1024, 1024), BF16),
            pltpu.VMEM((CAPR, 4096), BF16),
            pltpu.VMEM((1024, 2048), BF16),
            pltpu.VMEM((KW, 1024), BF16),
            pltpu.VMEM((1024, 1024), BF16),
            pltpu.VMEM((1024, 1024), BF16),
            pltpu.VMEM((8, TILE), F32),
            pltpu.VMEM((1024, 512), F32),
            pltpu.VMEM((304, TILE), F32),
            pltpu.VMEM((40, TILE), F32),
            pltpu.VMEM((72, TILE), F32),
            pltpu.VMEM((9, 72, TILE), F32),
            pltpu.VMEM((256, TILE), F32),
            pltpu.VMEM((1024, 2048), BF16),
            pltpu.VMEM((16, 192, TILE), BF16),
            pltpu.VMEM((16, 192, TILE), BF16),
            pltpu.VMEM((512, 16 * CAPR), BF16),
            pltpu.VMEM((CHUNKS, 2, 256, 256), F32),
            pltpu.VMEM((CHUNKS, 2, 256, 256), BF16),
            pltpu.VMEM((CHUNKS, 256, 256), BF16),
            pltpu.VMEM((CHUNKS, 8, 32, 256), BF16),
            pltpu.VMEM((CHUNKS, 8, 32, 256), BF16),
            pltpu.VMEM((CHUNKS, 2, 32, TILE), BF16),
            dma((22,)), dma((4,)),
            dma((CHUNKS, 16)), dma((CHUNKS, 16)),
            dma((CHUNKS,)), dma((CHUNKS,)),
            dma((CHUNKS, 8)), dma((CHUNKS, 8)),
            dma((CHUNKS, 16)), dma((CHUNKS, 16)),
        ],
        compiler_params=pltpu.CompilerParams(
            collective_id=0, has_side_effects=True, vmem_limit_bytes=56 * 2**20
        ),
    )(
        lengths, routes.T, frames, hidden_grad, pw_weight, dw_kernel, conv_grad
    )
    return pl.pallas_call(
        finish,
        out_shape=(
            jax.ShapeDtypeStruct((1024, 1024), BF16),
            jax.ShapeDtypeStruct((CAP, 64, TILE), F32),
        ),
        in_specs=[hbm] * 3,
        out_specs=(hbm, hbm),
        scratch_shapes=[
            pltpu.SMEM((32,), I32),
            pltpu.SMEM((33,), I32),
            pltpu.VMEM((1024, 1024), BF16),
            pltpu.VMEM((CAP, 2, 32, TILE), BF16),
            pltpu.VMEM((CAP, 64, TILE), F32),
            dma, dma((2, 4)), dma((CAP, 2)), dma,
        ],
        compiler_params=pltpu.CompilerParams(vmem_limit_bytes=56 * 2**20),
    )(owners.reshape(32), grad, gathered)


def solution(mesh):
    in_specs = (
        P(("node", "local"), None),
        P(("node", "local"), None),
        P(("node", "local"), None),
        P(),
        P(),
        P(),
        P(("node", "local"), None),
        P(("node", "local"), None, None),
    )
    out_specs = (P(("node", "local"), None), P("node", "local", None))
    return jax.shard_map(shards, mesh=mesh, in_specs=in_specs, out_specs=out_specs, check_vma=False)
```

```python
import functools

import jax
import jax.numpy as jnp
from jax import lax
from jax.experimental import pallas as pl
from jax.experimental.pallas import tpu as pltpu
from jax.sharding import PartitionSpec as P

MESH = pl.DeviceIdType.MESH
F32, BF16, I32 = jnp.float32, jnp.bfloat16, jnp.int32

TILE = 128
UTT_LEN = 256
KW = 31
FAR_FIRST = sorted(range(1, 16), key=lambda o: -min(o // 4, 4 - o // 4) - min(o % 4, 4 - o % 4))
CAPR = 24
CHUNKS = 2
CAP = 6


def kernel(
    slots,
    lengths_hbm, routes_hbm, frames, hidden, weight, taps_hbm, conv_grad,
    out, gathered,
    lengths, routes, frames_v, hidden_v, weight_v, taps_v, conv_v, out_v,
    flags, glu, padded, taps_f, coef, phase, conv_back, dproj,
    send1, recv1, left_t, piece, piece_b, recv2, half_b, recv3, total_b,
    load_sem, store_sem,
    send1_sem, recv1_sem, send2_sem, recv2_sem, send3_sem, recv3_sem, send4_sem, recv4_sem,
):
    node, local = lax.axis_index("node"), lax.axis_index("local")
    z, core = local // 2, local % 2
    partner = local + 1 - 2 * core
    y, x = node // 4, node % 4

    barrier = pltpu.get_barrier_semaphore()

    def greet(o, c):
        pl.semaphore_signal(barrier, inc=1, device_id=((node + o) % 16, local), device_id_type=MESH)
        return c

    def greet_z(o, c):
        pl.semaphore_signal(
            barrier, inc=1, device_id=(node, (z + o) % 8 * 2 + core), device_id_type=MESH
        )
        return c

    lax.fori_loop(1, 16, greet, 0)
    lax.fori_loop(1, 8, greet_z, 0)
    pl.semaphore_signal(barrier, inc=1, device_id=(node, partner), device_id_type=MESH)

    def load(source, target, i):
        return pltpu.make_async_copy(source, target, load_sem.at[i])

    def load_weight(cb, part):
        start = pl.multiple_of(cb * TILE, TILE)
        return load(
            weight.at[:, pl.ds(part * 1024 + start, TILE)],
            weight_v.at[:, pl.ds(pl.multiple_of(cb * 256, 256) + part * TILE, TILE)],
            4 + cb * 2 + part,
        )

    load_frames = [
        load(frames.at[pl.ds(i * 256, 256)], frames_v.at[pl.ds(i * 256, 256)], 22 + i) for i in range(4)
    ]
    load_hidden = load(hidden.at[0], hidden_v, 1)
    load_taps = load(taps_hbm, taps_v, 2)
    load_conv = load(conv_grad, conv_v, 3)
    load_lengths = load(lengths_hbm, lengths, 20)
    load_routes = load(routes_hbm, routes, 21)
    load_routes.start()
    load_lengths.start()
    for part in load_frames:
        part.start()
    load_hidden.start()
    load_weight(0, 0).start()
    load_weight(0, 1).start()
    load_weight(1, 0).start()
    load_weight(1, 1).start()
    load_taps.start()
    load_conv.start()

    load_routes.wait()
    load_lengths.wait()
    lane = lax.broadcasted_iota(I32, (1, TILE), 1)
    for r in range(8):
        named = routes[:, r * TILE:(r + 1) * TILE] == 0
        named = jnp.max(named.astype(I32), axis=0, keepdims=True)
        valid = lane + (r % 2) * TILE < lengths[0, r // 2]
        flags[r:r + 1, :] = jnp.where(valid, named, 0).astype(F32)
    routed = flags[...]
    upto = (
        lax.broadcasted_iota(I32, (TILE, TILE), 0) <= lax.broadcasted_iota(I32, (TILE, TILE), 1)
    ).astype(F32)
    before = (
        lax.broadcasted_iota(I32, (8, 8), 1) < lax.broadcasted_iota(I32, (8, 8), 0)
    ).astype(F32)
    in_row = jnp.dot(routed, upto, preferred_element_type=F32)
    row_sum = jnp.broadcast_to(jnp.sum(routed, axis=1, keepdims=True), (8, TILE))
    order = in_row + jnp.dot(before, row_sum, preferred_element_type=F32)
    flags[...] = jnp.where(routed > 0, order - 1.0, -1.0)
    want = lax.broadcasted_iota(I32, (32, TILE), 0).astype(F32)
    chosen = jnp.concatenate(
        [(jnp.broadcast_to(flags[r:r + 1, :], (32, TILE)) == want).astype(F32) for r in range(8)], axis=1
    ).astype(BF16)
    slot = jnp.zeros((32, 1024), F32)
    for i in range(4):
        load_frames[i].wait()
        part = pl.ds(i * 256, 256)
        slot = slot + jnp.dot(chosen[:, i * 256:(i + 1) * 256], frames_v[part, :], preferred_element_type=F32)
    slot = slot[0:CAPR]

    group = lax.broadcasted_iota(I32, (CAPR, TILE), 1) // 32
    sets = []
    for g in range(2):
        tiles = []
        for c in range(2):
            for half in range(2):
                tile = None
                for i in range(4):
                    zz = half * 4 + i
                    part = pltpu.roll(slot[:, zz * TILE:(zz + 1) * TILE], ((i - (2 * c + g)) * 32) % TILE, 1)
                    tile = part if tile is None else jnp.where(group == i, part, tile)
                tiles.append(tile)
        sets.append(jnp.concatenate(tiles, axis=0).astype(BF16))
    load_hidden.wait()
    for m in range(8):
        columns = [
            hidden_v[:, (m * 4 + t) * TILE:(m * 4 + t + 1) * TILE].astype(F32) for t in range(4)
        ]
        columns = jnp.concatenate(columns, axis=0).astype(BF16)
        for g in range(2):
            send1[g * 8 + m, 0:96, :] = sets[g]
            send1[g * 8 + m, 96:192, :] = columns
    recv1[node] = send1[node]

    pl.semaphore_wait(barrier, 23)

    rows1 = ((0, 144), (144, 48))

    def copy1(chunk, o):
        to = (y + o // 4) % 4 * 4 + (x + o % 4) % 4
        rows = pl.ds(*rows1[chunk])
        return pltpu.make_async_remote_copy(
            src_ref=send1.at[to, rows], dst_ref=recv1.at[node, rows],
            send_sem=send1_sem.at[chunk, o], recv_sem=recv1_sem.at[chunk, o],
            device_id=(to, local), device_id_type=MESH,
        )

    def copy2(chunk):
        return pltpu.make_async_remote_copy(
            src_ref=piece_b.at[chunk, 1 - core], dst_ref=recv2.at[chunk],
            send_sem=send2_sem.at[chunk], recv_sem=recv2_sem.at[chunk],
            device_id=(node, partner), device_id_type=MESH,
        )

    def copy3(chunk, o):
        to = (z + o) % 8
        return pltpu.make_async_remote_copy(
            src_ref=half_b.at[chunk, to], dst_ref=recv3.at[chunk, z],
            send_sem=send3_sem.at[chunk, o], recv_sem=recv3_sem.at[chunk, o],
            device_id=(node, to * 2 + core), device_id_type=MESH,
        )

    def copy4(chunk, o):
        to = (y + o // 4) % 4 * 4 + (x + o % 4) % 4
        return pltpu.make_async_remote_copy(
            src_ref=total_b.at[chunk], dst_ref=gathered.at[node, pl.ds(2 * chunk, 2)],
            send_sem=send4_sem.at[chunk, o], recv_sem=recv4_sem.at[chunk, o],
            device_id=(to, local), device_id_type=MESH,
        )

    def keep_own(chunk):
        return pltpu.make_async_copy(
            total_b.at[chunk], gathered.at[node, pl.ds(2 * chunk, 2)], load_sem.at[chunk]
        )

    def each(count, do):
        def step(o, c):
            do(o)
            return c

        lax.fori_loop(1, count, step, 0)

    for o in FAR_FIRST:
        copy1(0, o).start()
    for cb in range(2, 8):
        load_weight(cb, 0).start()
        load_weight(cb, 1).start()


    def send_rest():
        each(16, lambda o: copy1(0, o).wait_send())
        for o in FAR_FIRST:
            copy1(1, o).start()

    def multiply(chunk):
        each(16, lambda o: copy1(chunk, o).wait_recv())

        def tiles(first, count):
            rows = recv1[:, first * CAPR:(first + count) * CAPR, :].astype(F32)
            rows = rows.reshape(16, count, CAPR, TILE)
            parts = [rows[:, t].reshape(16 * CAPR, TILE) for t in range(count)]
            return jnp.concatenate(parts, axis=1).astype(BF16)

        if chunk == 0:
            left_t[...] = tiles(0, 4).T
        both = jnp.dot(left_t[...], tiles(4 + 2 * chunk, 2), preferred_element_type=F32)
        both = both.reshape(2, 256, 256)
        piece[chunk] = both
        piece_b[chunk] = both.astype(BF16)
        copy2(chunk).start()

    def add_cores(chunk):
        copy2(chunk).wait_recv()
        half = piece[chunk, core] + recv2[chunk].astype(F32)
        half_b[chunk] = half.astype(BF16).reshape(8, 32, 256)
        recv3[chunk, z] = half_b[chunk, z]
        for o in (4, 3, 5, 2, 6, 1, 7):
            copy3(chunk, o).start()

    def add_chips(chunk):
        each(8, lambda o: copy3(chunk, o).wait_recv())
        total = recv3[chunk, 0].astype(F32)
        for other in range(1, 8):
            total = total + recv3[chunk, other].astype(F32)
        total = total.astype(BF16)
        for t in range(2):
            total_b[chunk, t] = total[:, t * TILE:(t + 1) * TILE]
        for o in FAR_FIRST:
            copy4(chunk, o).start()
        keep_own(chunk).start()

    steps = {
        slots[6]: send_rest,
        slots[0]: lambda: multiply(0),
        slots[1]: lambda: multiply(1),
        slots[2]: lambda: add_cores(0),
        slots[3]: lambda: add_cores(1),
        slots[4]: lambda: add_chips(0),
        slots[5]: lambda: add_chips(1),
    }

    def hook(now):
        for at, step in steps.items():
            pl.when(now == at)(step)

    padded[0:16, :] = jnp.zeros((16, TILE), F32)
    padded[272:304, :] = jnp.zeros((32, TILE), F32)
    taps_f[...] = jnp.zeros((40, TILE), F32)
    load_taps.wait()
    load_conv.wait()
    R = 64
    Q = UTT_LEN // 4

    def coefficients(cb):
        taps_f[1:KW + 1, :] = taps_v[:, pl.ds(pl.multiple_of(cb * TILE, TILE), TILE)].astype(F32)
        u0, u1, u2, u3 = (taps_f[pl.ds(3 - m, 8, stride=4), :] for m in range(4))
        filters = (u0 + u1 + u2 + u3, u0 + u1, u2 + u3, u0 + u2, u0, u2, u1 + u3, u1, u3)
        for i, rows in enumerate(filters):
            coef[i * 8:i * 8 + 8, :] = rows

    def conv_tile(u, cb, at):
        rows_u = pl.multiple_of(u * UTT_LEN, UTT_LEN)
        lanes = pl.ds(pl.multiple_of(cb * TILE, TILE), TILE)
        valid = lax.broadcasted_iota(I32, (UTT_LEN, TILE), 0) < lengths[0, u]
        padded[16:272, :] = jnp.where(valid, conv_v[pl.ds(rows_u, UTT_LEN), lanes].astype(F32), 0.0)
        x0, x1, x2, x3, x4, x5, x6 = (padded[pl.ds(1 + m, Q + 8, stride=4), :] for m in range(7))
        d0, d1, d2 = x0 - x1, x2 - x3, x4 - x5
        e0, e1, e2 = x2 - x1, x4 - x3, x6 - x5
        inputs = (x3, x1 - x3, x5 - x3, d1, d0 - d1, d2 - d1, e1, e0 - e1, e2 - e1)
        for i, rows in enumerate(inputs):
            phase[i] = rows

        def correlate(i):
            acc = None
            for j in range(8):
                term = coef[i * 8 + 7 - j:i * 8 + 8 - j, :] * phase[i, j:j + Q, :]
                acc = term if acc is None else acc + term
            return acc

        q0, q1, q2 = correlate(0), correlate(1), correlate(2)
        qa, qb = q0 + q1, q0 + q2
        r0, r1, r2 = correlate(3), correlate(4), correlate(5)
        conv_back[pl.ds(0, Q, stride=4), :] = qa + (r0 + r1)
        conv_back[pl.ds(2, Q, stride=4), :] = qb + (r0 + r2)
        t0, t1, t2 = correlate(6), correlate(7), correlate(8)
        conv_back[pl.ds(1, Q, stride=4), :] = qa + (t0 + t1)
        conv_back[pl.ds(3, Q, stride=4), :] = qb + (t0 + t2)
        for r in range(UTT_LEN // R):
            rows = pl.ds(pl.multiple_of(rows_u + r * R, R), R)
            acc = jnp.where(valid[r * R:(r + 1) * R], conv_back[r * R:(r + 1) * R, :], 0.0)
            value, gate = glu[rows, pl.ds(at, TILE)], glu[rows, pl.ds(at + TILE, TILE)]
            sig = jax.nn.sigmoid(gate)
            d_value = acc * sig
            d_gate = d_value * value * (1.0 - sig)
            to = pl.multiple_of(cb * 256, 256)
            dproj[rows, pl.ds(to, TILE)] = d_value.astype(BF16)
            dproj[rows, pl.ds(to + TILE, TILE)] = d_gate.astype(BF16)

    def channels(pair, c):
        columns = pl.ds(pl.multiple_of(pair * 512, 512), 512)
        for t in range(2):
            for part in range(2):
                load_weight(pair * 2 + t, part).wait()
        glu[...] = jnp.dot(frames_v[...], weight_v[:, columns], preferred_element_type=F32)

        def one(t, c):
            coefficients(pair * 2 + t)

            def utterance(u, c):
                conv_tile(u, pair * 2 + t, pl.multiple_of(t * 256, 256))
                hook(pair * 8 + t * 4 + u)
                return c

            return lax.fori_loop(0, 4, utterance, c)

        return lax.fori_loop(0, 2, one, c)

    lax.fori_loop(0, 4, channels, 0)

    def quarter(i):
        rows = pl.ds(pl.multiple_of(i % 2 * 512, 512), 512)
        return rows, pl.ds(pl.multiple_of(i // 2 * 512, 512), 512)

    def store(i):
        part = quarter(i)
        return pltpu.make_async_copy(out_v.at[*part], out.at[*part], store_sem.at[i])

    def back(i, c):
        rows, columns = quarter(i)
        out_v[rows, columns] = lax.dot_general(
            dproj[rows, :], weight_v[columns, :], (((1,), (1,)), ((), ())), preferred_element_type=F32
        ).astype(BF16)
        store(i).start()
        hook(32 + i)
        return c

    lax.fori_loop(0, 4, back, 0)

    each(16, lambda o: copy1(1, o).wait_send())
    for chunk in range(CHUNKS):
        copy2(chunk).wait_send()
        each(8, lambda o: copy3(chunk, o).wait_send())
        keep_own(chunk).wait()
    for i in range(4):
        store(i).wait()
    for chunk in range(CHUNKS):
        each(16, lambda o: copy4(chunk, o).wait_send())
    for chunk in range(CHUNKS):
        each(16, lambda o: copy4(chunk, o).wait_recv())


def finish(owners_hbm, grad, gathered, out, owned, owners, picks, through, blocks, owned_v, owners_sem, move_sem, block_sem, owned_sem):
    node = lax.axis_index("node")

    def move_in(i):
        rows = pl.ds(i * 256, 256)
        return pltpu.make_async_copy(grad.at[rows], through.at[rows], move_sem.at[0, i])

    def move_out(i):
        rows = pl.ds(i * 256, 256)
        return pltpu.make_async_copy(through.at[rows], out.at[rows], move_sem.at[1, i])

    load_owners = pltpu.make_async_copy(owners_hbm, owners, owners_sem)
    load_owners.start()
    for i in range(4):
        move_in(i).start()
    load_owners.wait()
    held = jnp.int32(0)
    for i in range(32):
        picks[held] = jnp.int32(i)
        held = held + (owners[i] == node).astype(I32)

    def fetch(k, g):
        block = jnp.where(k < held, picks[k], 0)
        return pltpu.make_async_copy(
            gathered.at[g * 8 + block // 4, block % 4], blocks.at[k, g], block_sem.at[k, g]
        )

    for k in range(CAP):
        for g in range(2):
            fetch(k, g).start()
    for i in range(4):
        move_in(i).wait()
        move_out(i).start()
    for k in range(CAP):
        keep = jnp.broadcast_to(k < held, (32, TILE))
        for g in range(2):
            fetch(k, g).wait()
            owned_v[k, g * 32:(g + 1) * 32, :] = jnp.where(keep, blocks[k, g].astype(F32), 0.0)
    last = pltpu.make_async_copy(owned_v, owned, owned_sem)
    last.start()
    for i in range(4):
        move_out(i).wait()
    last.wait()


SLOTS = (15, 21, 18, 25, 28, 32, 12)


def shards(frames, lengths, routes, owners, pw_weight, dw_kernel, conv_grad, hidden_grad):
    hbm = pl.BlockSpec(memory_space=pl.ANY)
    dma = pltpu.SemaphoreType.DMA
    grad, gathered = pl.pallas_call(
        functools.partial(kernel, SLOTS),
        out_shape=(
            jax.ShapeDtypeStruct((1024, 1024), BF16),
            jax.ShapeDtypeStruct((16, 4, 32, TILE), BF16),
        ),
        in_specs=[hbm] * 7,
        out_specs=(hbm, hbm),
        scratch_shapes=[
            pltpu.SMEM((1, 4), I32),
            pltpu.VMEM((2, 1024), I32),
            pltpu.VMEM((1024, 1024), BF16),
            pltpu.VMEM((CAPR, 4096), BF16),
            pltpu.VMEM((1024, 2048), BF16),
            pltpu.VMEM((KW, 1024), BF16),
            pltpu.VMEM((1024, 1024), BF16),
            pltpu.VMEM((1024, 1024), BF16),
            pltpu.VMEM((8, TILE), F32),
            pltpu.VMEM((1024, 512), F32),
            pltpu.VMEM((304, TILE), F32),
            pltpu.VMEM((40, TILE), F32),
            pltpu.VMEM((72, TILE), F32),
            pltpu.VMEM((9, 72, TILE), F32),
            pltpu.VMEM((256, TILE), F32),
            pltpu.VMEM((1024, 2048), BF16),
            pltpu.VMEM((16, 192, TILE), BF16),
            pltpu.VMEM((16, 192, TILE), BF16),
            pltpu.VMEM((512, 16 * CAPR), BF16),
            pltpu.VMEM((CHUNKS, 2, 256, 256), F32),
            pltpu.VMEM((CHUNKS, 2, 256, 256), BF16),
            pltpu.VMEM((CHUNKS, 256, 256), BF16),
            pltpu.VMEM((CHUNKS, 8, 32, 256), BF16),
            pltpu.VMEM((CHUNKS, 8, 32, 256), BF16),
            pltpu.VMEM((CHUNKS, 2, 32, TILE), BF16),
            dma((26,)), dma((4,)),
            dma((CHUNKS, 16)), dma((CHUNKS, 16)),
            dma((CHUNKS,)), dma((CHUNKS,)),
            dma((CHUNKS, 8)), dma((CHUNKS, 8)),
            dma((CHUNKS, 16)), dma((CHUNKS, 16)),
        ],
        compiler_params=pltpu.CompilerParams(
            collective_id=0, has_side_effects=True, vmem_limit_bytes=56 * 2**20
        ),
    )(
        lengths, routes.T, frames, hidden_grad, pw_weight, dw_kernel, conv_grad
    )
    return pl.pallas_call(
        finish,
        out_shape=(
            jax.ShapeDtypeStruct((1024, 1024), BF16),
            jax.ShapeDtypeStruct((CAP, 64, TILE), F32),
        ),
        in_specs=[hbm] * 3,
        out_specs=(hbm, hbm),
        scratch_shapes=[
            pltpu.SMEM((32,), I32),
            pltpu.SMEM((33,), I32),
            pltpu.VMEM((1024, 1024), BF16),
            pltpu.VMEM((CAP, 2, 32, TILE), BF16),
            pltpu.VMEM((CAP, 64, TILE), F32),
            dma, dma((2, 4)), dma((CAP, 2)), dma,
        ],
        compiler_params=pltpu.CompilerParams(vmem_limit_bytes=56 * 2**20),
    )(owners.reshape(32), grad, gathered)


def solution(mesh):
    in_specs = (
        P(("node", "local"), None),
        P(("node", "local"), None),
        P(("node", "local"), None),
        P(),
        P(),
        P(),
        P(("node", "local"), None),
        P(("node", "local"), None, None),
    )
    out_specs = (P(("node", "local"), None), P("node", "local", None))
    return jax.shard_map(shards, mesh=mesh, in_specs=in_specs, out_specs=out_specs, check_vma=False)
```
